32 devices in a mesh: group: 2 (over x), clus: 16 (over z, y, core).
Axes of the slice: x: 2, y: 2, z: 4, core: 2. Of those that a mesh axis runs over, the one named last changes fastest.
Arguments:
- block_vectors: float32 [512, 32, 256], P(('group', 'clus')), parts along dimension 0, may hold values from -6 to 6
- prior_vectors: float32 [512, 32, 256], P(('group', 'clus')), parts along dimension 0, may hold values from -6 to 6
- prior_beta: float32 [64, 32], P('group'), parts along dimension 0, may hold values from -1.2 to 1.2
- points: bfloat16 [512, 3, 256], P(('group', 'clus')), parts along dimension 0, may hold values from 0 to 1.3
- basis: bfloat16 [512, 32, 256], P(('group', 'clus')), parts along dimension 0, may hold values from -0.375 to 0.375
- scales: float32 [512, 32], P(('group', 'clus')), parts along dimension 0, may hold values from 0.5 to 2
- skeleton: bfloat16 [512, 3, 32], P(('group', 'clus')), parts along dimension 0, may hold values from 0 to 1.3
- near_pairs: int32 [32, 16, 3, 2], P(('group', 'clus')), parts along dimension 0, may hold values from -1 to 15, as said below
- far_ids: int32 [512, 64], P(('group', 'clus')), parts along dimension 0, may hold values from 0 to 255
Outputs:
- next_vectors: float32 [512, 32, 256], P(('group', 'clus')), parts along dimension 0
- alpha_block: float32 [64, 32], P('group'), parts along dimension 0
- beta_block: float32 [64, 32], P('group'), parts along dimension 0
The draws below stay inside these ranges and needn't reach their ends.
There are 2 independent parts, one for each index of `group`. The reference program is written for one: setup_inputs(seed, part) draws one part's arguments, and reference() takes and returns one part's arrays. A program takes and returns all parts, laid end to end along the dimension named above; each array names one. Nothing has to cross between parts.
Inputs may be any that keep to these rules, and one draw needn't show every extreme that they name: near_pairs[o, p, t, 0] is -1 for an empty entry, else a row cluster index local to device o; near_pairs[o, p, t, 1] is a cluster index local to device p and differs from near_pairs[o, p, t, 0]. The share of live entries differs from device to device; in every draw all entries of some device are live.
All inputs are finite; a program needn't handle non-finite values.
Results may differ from the reference program's by a relative error of at most 0.0045.
Values may be sent and summed in bfloat16 or wider, within the bound.
No kernel may reach another device: no remote copies, remote signals or barrier semaphores. Data moves between devices by JAX's collectives and lax.ppermute only.
A program may use at most 128 MiB of HBM per device.

```python
import math
import jax
import jax.numpy as jnp
from jax import lax

CSIZE = 256
VEC = 32
RANK = 32
CL_DEV = 16
SLOT = 3
FAR = 64
CLUSTERS = 256
POINTS = 65536
N_CLUS = 16


def draw_points(key, part):
    key = jax.random.fold_in(key, 11)
    offset_key, cloud_key = jax.random.split(key)
    offsets = jax.random.uniform(offset_key, (CLUSTERS, 3, 1), jnp.float32, 0.0, 0.3)
    cloud_points = jax.random.uniform(cloud_key, (CLUSTERS, 3, CSIZE), jnp.float32, 0.0, 1.0)
    return (offsets + cloud_points).astype(jnp.bfloat16)


def draw_skeleton(key, part):
    key = jax.random.fold_in(key, 17)
    offset_key, cloud_key = jax.random.split(key)
    offsets = jax.random.uniform(offset_key, (CLUSTERS, 3, 1), jnp.float32, 0.0, 0.3)
    cloud_points = jax.random.uniform(cloud_key, (CLUSTERS, 3, RANK), jnp.float32, 0.0, 1.0)
    return (offsets + cloud_points).astype(jnp.bfloat16)


def draw_near_pairs(key, part):
    key = jax.random.fold_in(key, 23)
    subkeys = jax.random.split(key, 5)
    levels = jax.random.randint(subkeys[0], (N_CLUS,), 1, 9)
    busiest = jax.random.randint(subkeys[1], (), 0, N_CLUS)
    levels = jnp.where(jnp.arange(N_CLUS) == busiest, 8, levels)
    trials = jax.random.randint(subkeys[2], (N_CLUS, N_CLUS, SLOT), 0, 8)
    live_mask = trials < levels[:, None, None]
    base_rows = jax.random.randint(subkeys[3], (N_CLUS, N_CLUS, SLOT), 0, CL_DEV)
    offset_rows = jax.random.randint(subkeys[4], (N_CLUS, N_CLUS, SLOT), 1, CL_DEV)
    row_index = jnp.where(live_mask, base_rows, -1)
    partner_index = (base_rows + offset_rows) % CL_DEV
    return jnp.stack([row_index, partner_index], axis=-1).astype(jnp.int32)


def with_ends(result, rng, low, largest):
    spot = [jax.random.randint(jax.random.fold_in(rng, axis), (), 0, length) for axis, length in enumerate(result.shape)]
    longest = result.shape.index(max(result.shape))
    neighbour = spot[:longest] + [(spot[longest] + 1) % result.shape[longest]] + spot[longest + 1:]
    return result.at[tuple(spot)].set(low).at[tuple(neighbour)].set(largest)


def level_of(own_key, dims, pieces, smallest, high):
    gain, own = 1.0, jax.random.fold_in(own_key, 6)
    for position, blocks in pieces:
        draws = jnp.exp(jax.random.uniform(jax.random.fold_in(own, position), (blocks,), jnp.float32, smallest / len(pieces), high / len(pieces)))
        gain = gain * jnp.repeat(draws, dims[position] // blocks).reshape([-1 if axis == position else 1 for axis in range(len(dims))])
    return gain


def normal_values(key, dims, scale, most, cuts=(), held_as=jnp.bfloat16):
    values = jax.random.normal(key, dims, jnp.float32) * scale
    if len(cuts) > 0:
        values = level_of(key, dims, cuts, -0.22, 0.18) * values
    return jnp.clip(values, min=-most, max=most).astype(held_as)


def setup_inputs(seed: int = 0, part: int = 0) -> dict:
    splits = jax.random.split(jax.random.key(seed), 10)
    own_keys = jax.random.split(jax.random.fold_in(splits[9], part), 10)
    block_vectors = normal_values(own_keys[0], (CLUSTERS, VEC, CSIZE), 1.0, 6.0, ((0, 16),), jnp.float32)
    prior_vectors = normal_values(own_keys[1], (CLUSTERS, VEC, CSIZE), 1.0, 6.0, ((0, 16),), jnp.float32)
    prior_beta = normal_values(own_keys[2], (VEC, VEC), 0.2, 1.2, (), jnp.float32)
    points = draw_points(jax.random.fold_in(jax.random.fold_in(splits[9], part), 71), part)
    basis = normal_values(own_keys[4], (CLUSTERS, RANK, CSIZE), CSIZE ** -0.5, 0.375, ((0, 16),))
    scales = jnp.clip(jnp.exp(math.log(2.0) - 1.3862944 * jax.random.uniform(own_keys[5], (CLUSTERS, RANK), jnp.float32) ** level_of(own_keys[5], (CLUSTERS, RANK), ((0, 16),), -0.2, 0.2)), 0.5, 2.0)
    skeleton = draw_skeleton(jax.random.fold_in(jax.random.fold_in(splits[9], part), 71), part)
    near_pairs = draw_near_pairs(jax.random.fold_in(jax.random.fold_in(splits[9], part), 71), part)
    far_ids = with_ends(jax.random.randint(own_keys[8], (CLUSTERS, FAR), 0, CLUSTERS), jax.random.fold_in(own_keys[8], 1), 0, CLUSTERS - 1).astype(jnp.int32)
    return {"block_vectors": block_vectors, "prior_vectors": prior_vectors, "prior_beta": prior_beta, "points": points, "basis": basis, "scales": scales, "skeleton": skeleton, "near_pairs": near_pairs, "far_ids": far_ids}


root_three = 1.7320508075688772
length_scale = 0.15

def kernel_tile(left_points, right_points):
    left_wide = left_points.astype(jnp.float32)
    right_wide = right_points.astype(jnp.float32)
    difference = left_wide[..., 0, :, None] - right_wide[..., 0, None, :]
    squared = difference * difference
    for coordinate in range(1, 3):
        difference = left_wide[..., coordinate, :, None] - right_wide[..., coordinate, None, :]
        squared = squared + difference * difference
    scaled = jnp.sqrt(squared) * (root_three / length_scale)
    return (1.0 + scaled) * jnp.exp(-scaled)

def to_half(values):
    return lax.optimization_barrier(values.astype(jnp.bfloat16)).astype(jnp.float32)

def reference(block_vectors, prior_vectors, prior_beta, points, basis, scales, skeleton, near_pairs, far_ids):
    highest = lax.Precision.HIGHEST
    half_wide = to_half(block_vectors)
    basis_wide = basis.astype(jnp.float32)
    vec_count = block_vectors.shape[1]
    group_ids = jnp.arange(N_CLUS, dtype=jnp.int32)

    def self_block(owner_index):
        first_row = owner_index * CL_DEV
        mine_points = lax.dynamic_slice_in_dim(points, first_row, CL_DEV, 0)
        mine_vectors = lax.dynamic_slice_in_dim(half_wide, first_row, CL_DEV, 0)
        self_tiles = to_half(kernel_tile(mine_points, mine_points))
        return jnp.einsum('cvb,cba->cva', mine_vectors, self_tiles, precision=highest)
    self_term = lax.map(self_block, group_ids).reshape(block_vectors.shape)
    peer_ids = jnp.repeat(jnp.arange(N_CLUS, dtype=jnp.int32), SLOT)

    def near_owner(applied, owner_index):
        entries = lax.dynamic_index_in_dim(near_pairs, owner_index, 0, keepdims=False).reshape(N_CLUS * SLOT, 2)
        live_mask = entries[:, 0] >= 0
        row_ids = owner_index * CL_DEV + jnp.maximum(entries[:, 0], 0)
        partner_ids = peer_ids * CL_DEV + entries[:, 1]
        kernel_tiles = to_half(kernel_tile(points[partner_ids], points[row_ids]))
        weight = live_mask.astype(jnp.float32)[:, None, None]
        direct = jnp.einsum('svb,sba->sva', half_wide[partner_ids], kernel_tiles, precision=highest) * weight
        mirror = to_half(jnp.einsum('sva,sba->svb', half_wide[row_ids], kernel_tiles, precision=highest)) * weight
        applied = applied.at[row_ids].add(direct).at[partner_ids].add(mirror)
        return (applied, None)
    near_term, unused = lax.scan(near_owner, jnp.zeros(block_vectors.shape, jnp.float32), group_ids)
    projected = jnp.einsum('crb,cvb->crv', basis_wide, half_wide, precision=highest)
    sources = to_half(scales[:, :, None] * projected)

    def far_block(owner_index):
        first_row = owner_index * CL_DEV
        far_rows = lax.dynamic_slice_in_dim(far_ids, first_row, CL_DEV, 0)
        mine_skeleton = lax.dynamic_slice_in_dim(skeleton, first_row, CL_DEV, 0)
        coupling = to_half(kernel_tile(mine_skeleton[:, None], skeleton[far_rows]))
        gathered = jnp.einsum('cfab,cfbv->cav', coupling, sources[far_rows], precision=highest)
        mine_scales = lax.dynamic_slice_in_dim(scales, first_row, CL_DEV, 0)
        lifted = to_half(mine_scales[:, :, None] * gathered)
        mine_basis = lax.dynamic_slice_in_dim(basis_wide, first_row, CL_DEV, 0)
        return jnp.einsum('crv,crb->cvb', lifted, mine_basis, precision=highest)
    far_term = lax.map(far_block, group_ids).reshape(block_vectors.shape)
    applied = self_term + near_term + far_term
    alpha_block = jnp.einsum('cub,cvb->uv', block_vectors, applied, precision=highest) / POINTS
    residual = applied - jnp.einsum('uv,cub->cvb', alpha_block, block_vectors, precision=highest)
    residual = residual - jnp.einsum('vu,cub->cvb', prior_beta, prior_vectors, precision=highest)
    gram_matrix = jnp.einsum('cub,cvb->uv', residual, residual, precision=highest) / POINTS
    factor = jnp.linalg.cholesky(gram_matrix)
    inverse = lax.linalg.triangular_solve(factor, jnp.eye(vec_count, dtype=jnp.float32), left_side=True, lower=True)
    next_vectors = jnp.einsum('uv,cvb->cub', inverse, residual, precision=highest)
    return (next_vectors, alpha_block, factor.T)
```

```python
import functools
import math

import jax
import jax.numpy as jnp
from jax import lax
from jax.experimental import pallas as pl
from jax.experimental.pallas import tpu as pltpu
from jax.sharding import PartitionSpec as P

root_three = 1.7320508075688772
length_scale = 0.15
steepness = root_three / length_scale
feature_count = 16
vmem_limit = 56 * 1024 * 1024
NT = (((1,), (1,)), ((), ()))


def kernel_values(squared):
    squared = jnp.maximum(squared, 1e-12)
    distance = squared * lax.rsqrt(squared)
    decay = jnp.exp2(distance * (-steepness * math.log2(math.e)))
    return (1.0 + distance * steepness) * decay


def dot_nt(left, right):
    return lax.dot_general(left, right, NT, preferred_element_type=jnp.float32)


def dot_exact(left, right, dims=(((1,), (0,)), ((), ()))):
    return lax.dot_general(
        left, right, dims, precision=lax.Precision.HIGHEST, preferred_element_type=jnp.float32
    )


def squared_distances(left_features, right_features):
    return jnp.dot(left_features, right_features, preferred_element_type=jnp.float32)


def tile_of(left_features, right_features):
    return kernel_values(squared_distances(left_features, right_features)).astype(jnp.bfloat16)


def features_of(coordinates):
    wide = coordinates.astype(jnp.float32)
    norm = jnp.sum(wide * wide, axis=-2, keepdims=True)
    high = lax.reduce_precision(norm, 8, 7)
    middle = lax.reduce_precision(norm - high, 8, 7)
    low = lax.reduce_precision(norm - high - middle, 8, 7)
    pieces = jnp.concatenate([high, middle, low], axis=-2)
    ones = jnp.ones_like(pieces)
    blank = jnp.zeros(norm.shape[:-2] + (feature_count - 9, norm.shape[-1]), jnp.float32)
    left = jnp.concatenate([wide, pieces, ones, blank], axis=-2).astype(jnp.bfloat16)
    right = jnp.concatenate([-2.0 * wide, ones, pieces, blank], axis=-2).astype(jnp.bfloat16)
    return left, right


def sources_kernel(half_ref, basis_ref, scales_ref, out_ref):
    clusters, rank, _ = basis_ref.shape
    per_row = out_ref.shape[2] // rank
    for cluster in range(clusters):
        projected = dot_nt(half_ref[cluster], basis_ref[cluster])
        scaled = projected * scales_ref[cluster : cluster + 1, :]
        first = (cluster % per_row) * rank
        out_ref[cluster // per_row, :, first : first + rank] = scaled.astype(jnp.bfloat16)


def local_kernel(
    half_ref, left_ref, right_ref, basis_ref, scales_ref, skel_left_ref, skel_right_ref,
    counts_ref, sources_ref, out_ref, gathered_ref
):
    clusters, vecs, size = half_ref.shape
    rank = basis_ref.shape[1]
    parts = sources_ref.shape[0]
    halves = gathered_ref.shape[0]
    per_half = clusters // halves

    def self_step(cluster, carry):
        tile = tile_of(left_ref[cluster], right_ref[cluster])
        out_ref[cluster] = dot_nt(half_ref[cluster], tile)
        return carry

    lax.fori_loop(0, clusters, self_step, 0)
    gathered_ref[...] = jnp.zeros_like(gathered_ref)

    def far_step(part, carry):
        part_features = skel_right_ref[part]
        part_sources = sources_ref[part]
        for side in range(halves):
            values = kernel_values(
                squared_distances(skel_left_ref[side], part_features)
            )
            weights = counts_ref[part, pl.ds(side * per_half, per_half), :]
            values = values.astype(jnp.bfloat16).astype(jnp.float32)
            values = values.reshape(per_half, rank, size) * weights[:, None, :]
            values = values.reshape(per_half * rank, size).astype(jnp.bfloat16)
            gathered_ref[side] += dot_nt(part_sources, values)
        return carry

    lax.fori_loop(0, parts, far_step, 0)
    for cluster in range(clusters):
        side, first = cluster // per_half, (cluster % per_half) * rank
        block = gathered_ref[side][:, first : first + rank]
        lifted = (block * scales_ref[cluster : cluster + 1, :]).astype(jnp.bfloat16)
        out_ref[cluster] += jnp.dot(
            lifted, basis_ref[cluster], preferred_element_type=jnp.float32
        )


def near_kernel(
    live_ref, source_ref, own_ref, mirror_ref, vectors_ref, right_ref, left_ref, local_ref,
    block_ref, prior_ref, beta_ref, stacked_ref, products_ref, total_ref
):
    clusters, vecs, size = local_ref.shape
    total_ref[:clusters] = local_ref[...]

    def entry(place):
        source = source_ref[place]
        own = own_ref[place]
        tile = tile_of(left_ref[own], right_ref[source])
        term = dot_nt(vectors_ref[source], tile)
        rounded = term.astype(jnp.bfloat16).astype(jnp.float32)
        return own, jnp.where(mirror_ref[place] > 0, rounded, term)

    def step(turn, carry):
        first_own, first_term = entry(2 * turn)
        second_own, second_term = entry(2 * turn + 1)
        total_ref[first_own] += first_term
        total_ref[second_own] += second_term
        return carry

    lax.fori_loop(0, lax.div(live_ref[0] + 1, 2), step, 0)
    beta = beta_ref[...]
    sums = jnp.zeros((2 * vecs, 3 * vecs), jnp.float32)
    for cluster in range(clusters):
        block = block_ref[cluster]
        applied = total_ref[cluster]
        shifted = applied - dot_exact(beta, prior_ref[cluster])
        stacked_ref[cluster, :vecs] = shifted
        stacked_ref[cluster, vecs:] = block
        sums += dot_exact(
            jnp.concatenate([block, shifted], axis=0),
            jnp.concatenate([applied, shifted, block], axis=0),
            NT,
        )
    products = jnp.concatenate(
        [sums[:vecs, : 2 * vecs], sums[vecs:, vecs : 2 * vecs], sums[:vecs, 2 * vecs :]], axis=1
    )
    for part in range(products_ref.shape[0]):
        products_ref[part] = products


def finish_kernel(point_count, products_ref, stacked_ref, next_ref, alpha_ref, beta_ref):
    clusters, vecs, size = next_ref.shape
    sums = products_ref[0]
    for part in range(1, products_ref.shape[0]):
        sums = sums + products_ref[part]
    sums = sums * (1.0 / point_count)
    alpha = sums[:, :vecs]
    crossed = sums[:, vecs : 2 * vecs]
    shifted = sums[:, 2 * vecs : 3 * vecs]
    block = sums[:, 3 * vecs :]
    alpha_ref[...] = alpha
    turned = alpha.T
    half_crossed = dot_exact(turned, crossed)
    gram = shifted - half_crossed - half_crossed.T
    gram = gram + dot_exact(turned, dot_exact(block, alpha))
    rows = lax.broadcasted_iota(jnp.int32, (vecs, vecs), 0)
    columns = lax.broadcasted_iota(jnp.int32, (vecs, vecs), 1)
    unit = (rows == columns).astype(jnp.float32)
    work = jnp.concatenate([gram, unit], axis=1)
    row_ids = lax.broadcasted_iota(jnp.int32, (vecs, 1), 0)
    for step in range(vecs - 1):
        pivot_row = work[step : step + 1, :]
        ratio = work[:, step : step + 1] * (1.0 / pivot_row[:, step : step + 1])
        work = work - jnp.where(row_ids > step, ratio, 0.0) * pivot_row
    pivots = jnp.sum(work[:, :vecs] * unit, axis=1, keepdims=True)
    work = work * (1.0 / jnp.sqrt(pivots))
    beta_ref[...] = jnp.where(columns >= rows, work[:, :vecs], 0.0)
    inverse = work[:, vecs:]
    joint = jnp.concatenate([inverse, -dot_exact(inverse, turned)], axis=1)
    for cluster in range(clusters):
        next_ref[cluster] = dot_exact(joint, stacked_ref[cluster])


def call(kernel, out_shape, operands, scratch=(), smem=0, flops=0):
    places = [pltpu.SMEM] * smem + [pltpu.VMEM] * (len(operands) - smem)
    return pl.pallas_call(
        kernel,
        out_shape=out_shape,
        in_specs=[pl.BlockSpec(memory_space=place) for place in places],
        out_specs=jax.tree.map(lambda _: pl.BlockSpec(memory_space=pltpu.VMEM), out_shape),
        scratch_shapes=list(scratch),
        compiler_params=pltpu.CompilerParams(vmem_limit_bytes=vmem_limit),
        cost_estimate=pl.CostEstimate(flops=flops, bytes_accessed=1 << 20, transcendentals=flops // 64),
    )(*operands)


def local(
    block_vectors, prior_vectors, prior_beta, points, basis, scales, skeleton, near_pairs, far_ids
):
    clusters, vecs, size = block_vectors.shape
    rank = basis.shape[1]
    parts = lax.axis_size("clus")
    me = lax.axis_index("clus")
    slots = near_pairs.shape[2]
    total_points = parts * clusters * size
    per_part = 2 * slots
    per_row = size // rank
    halves = clusters // per_row
    wide = functools.partial(jax.ShapeDtypeStruct, dtype=jnp.float32)
    narrow = functools.partial(jax.ShapeDtypeStruct, dtype=jnp.bfloat16)

    half_vectors = block_vectors.astype(jnp.bfloat16)
    all_vectors = lax.all_gather(
        half_vectors.reshape(clusters * vecs, size), "clus", axis=0, tiled=True
    ).reshape(parts * clusters, vecs, size)

    sources = call(
        sources_kernel, narrow((halves, vecs, size)), (half_vectors, basis, scales)
    )
    id_count = parts * per_part
    id_rows = -(-id_count // size)
    ids = jnp.pad(
        near_pairs.reshape(-1).astype(jnp.bfloat16), (0, id_rows * size - id_count)
    ).reshape(id_rows, size)
    skeleton_rows = skeleton.transpose(1, 0, 2).reshape(3 * halves, size)
    pieces = [
        sources.reshape(halves * vecs, size),
        points.reshape(clusters * 3, size),
        skeleton_rows,
        ids,
    ]
    starts = [0]
    for piece in pieces:
        starts.append(starts[-1] + piece.shape[0])
    padding = -starts[-1] % 8
    side = jnp.concatenate(pieces + [jnp.zeros((padding, size), jnp.bfloat16)], axis=0)
    sides = lax.all_gather(side, "clus", axis=0, tiled=False)
    all_sources, all_points, all_skeletons, all_ids = (
        sides[:, starts[k] : starts[k + 1]] for k in range(4)
    )
    all_sources = all_sources.reshape(parts * halves, vecs, size)
    all_points = all_points.reshape(parts * clusters, 3, size)
    all_skeletons = all_skeletons.reshape(parts, 3, halves, size).swapaxes(1, 2)
    all_skeletons = all_skeletons.reshape(parts * halves, 3, size)

    _, far_right = features_of(all_skeletons)
    own_skeleton = skeleton_rows.reshape(3, halves, size).swapaxes(0, 1)
    far_left = features_of(own_skeleton)[0].swapaxes(1, 2)
    own_left, own_right = features_of(points)
    own_left = own_left.swapaxes(1, 2)
    _, all_right = features_of(all_points)

    listed = far_ids[:, :, None] == jnp.arange(parts * clusters, dtype=jnp.int32)
    counts = jnp.sum(listed, axis=1).astype(jnp.float32)
    counts = jnp.repeat(counts, rank, axis=1)
    counts = counts.reshape(clusters, parts * halves, size).swapaxes(0, 1)
    local_part = call(
        local_kernel,
        wide((clusters, vecs, size)),
        (
            half_vectors, own_left, own_right, basis, scales, far_left, far_right,
            counts, all_sources,
        ),
        scratch=[pltpu.VMEM((halves, vecs, size), jnp.float32)],
        flops=1 << 32,
    )

    pairs = all_ids.reshape(parts, -1)[:, :id_count].astype(jnp.int32)
    pairs = pairs.reshape(parts, parts, slots, 2)
    peers = jnp.arange(parts, dtype=jnp.int32)[:, None] * clusters
    asked = near_pairs[0]
    told = lax.dynamic_index_in_dim(pairs, me, axis=1, keepdims=False)
    live = jnp.concatenate([asked[..., 0] >= 0, told[..., 0] >= 0], axis=0).reshape(-1)
    origin = jnp.concatenate([peers + asked[..., 1], peers + told[..., 0]], axis=0).reshape(-1)
    target = jnp.concatenate([asked[..., 0], told[..., 1]], axis=0).reshape(-1)
    mirror = jnp.concatenate([jnp.zeros_like(asked[..., 0]), jnp.ones_like(told[..., 0])], axis=0)
    place = jnp.where(live, jnp.cumsum(live.astype(jnp.int32)) - 1, id_count + 1)
    packed = jnp.stack([origin, target, mirror.reshape(-1)])
    chosen = place[None, :] == jnp.arange(id_count + 1, dtype=jnp.int32)[:, None]
    table = jnp.sum(jnp.where(chosen[None], packed[:, None, :], 0), axis=2)
    spare = jnp.logical_not(jnp.any(chosen, axis=1))
    live_count = jnp.sum(live.astype(jnp.int32)).reshape(1)
    stacked, products = call(
        near_kernel,
        (wide((clusters, 2 * vecs, size)), wide((parts, vecs, 4 * vecs))),
        (
            live_count, table[0], jnp.where(spare, clusters, table[1]), table[2],
            all_vectors, all_right,
            jnp.concatenate([own_left, own_left[:1]], axis=0), local_part,
            block_vectors, prior_vectors, prior_beta,
        ),
        scratch=[pltpu.VMEM((clusters + 1, vecs, size), jnp.float32)],
        smem=4,
        flops=1 << 31,
    )
    summed = lax.all_to_all(products, "clus", split_axis=0, concat_axis=0, tiled=True)
    return call(
        functools.partial(finish_kernel, total_points),
        (wide((clusters, vecs, size)), wide((vecs, vecs)), wide((vecs, vecs))),
        (summed, stacked),
    )


def solution(mesh):
    placed = (
        P(("group", "clus"), None, None),
        P(("group", "clus"), None, None),
        P("group", None),
        P(("group", "clus"), None, None),
        P(("group", "clus"), None, None),
        P(("group", "clus"), None),
        P(("group", "clus"), None, None),
        P(("group", "clus"), None, None, None),
        P(("group", "clus"), None),
    )
    return jax.shard_map(
        local,
        mesh=mesh,
        in_specs=placed,
        out_specs=(P(("group", "clus"), None, None), P("group", None), P("group", None)),
        check_vma=False,
    )
```

```python
import functools
import math

import jax
import jax.numpy as jnp
from jax import lax
from jax.experimental import pallas as pl
from jax.experimental.pallas import tpu as pltpu
from jax.sharding import PartitionSpec as P

root_three = 1.7320508075688772
length_scale = 0.15
steepness = root_three / length_scale
feature_count = 16
unroll = 8
NT = (((1,), (1,)), ((), ()))


def kernel_values(squared):
    squared = jnp.maximum(squared, 1e-12)
    distance = squared * lax.rsqrt(squared)
    decay = jnp.exp2(distance * (-steepness * math.log2(math.e)))
    return (1.0 + distance * steepness) * decay


def dot_nt(left, right):
    return lax.dot_general(left, right, NT, preferred_element_type=jnp.float32)


def dot_exact(left, right, dims=(((1,), (0,)), ((), ()))):
    return lax.dot_general(
        left, right, dims, precision=lax.Precision.HIGHEST, preferred_element_type=jnp.float32
    )


def split(values):
    high = values.astype(jnp.bfloat16)
    return high, (values - high.astype(jnp.float32)).astype(jnp.bfloat16)


def dot_split(left, right):
    left_high, left_low = split(left)
    right_high, right_low = split(right)
    return dot_nt(
        jnp.concatenate([left_high, left_high, left_low], axis=1),
        jnp.concatenate([right_high, right_low, right_high], axis=1),
    )


def values_of(left_features, right_features):
    return kernel_values(jnp.dot(left_features, right_features, preferred_element_type=jnp.float32))


def tile_of(left_features, right_features):
    return values_of(left_features, right_features).astype(jnp.bfloat16)


def norm_pieces(axes):
    norm = axes[0] * axes[0] + axes[1] * axes[1] + axes[2] * axes[2]
    high = norm.astype(jnp.bfloat16).astype(jnp.float32)
    rest = norm - high
    middle = rest.astype(jnp.bfloat16).astype(jnp.float32)
    return [high, middle, rest - middle]


def stack_rows(rows):
    rows = rows + [jnp.zeros_like(rows[0])] * (feature_count - len(rows))
    return jnp.transpose(jnp.stack(rows, axis=0), (1, 0, 2))


def left_rows(axes):
    one = jnp.ones_like(axes[0])
    return stack_rows(list(axes) + norm_pieces(axes) + [one, one, one])


def right_rows(axes):
    one = jnp.ones_like(axes[0])
    return stack_rows([-2.0 * axis for axis in axes] + [one, one, one] + norm_pieces(axes))


def layout_of(clusters, vecs, rank, size):
    halves = clusters * rank // size
    rows = {"sources": clusters * vecs}
    rows["points"] = rows["sources"] + halves * vecs
    rows["skeleton"] = rows["points"] + 3 * clusters
    rows["ids"] = -(-(rows["skeleton"] + 3 * halves) // 8) * 8
    rows["end"] = -(-(rows["ids"] + 8) // 16) * 16
    return rows


def prepare_kernel(
    rows, block_ref, basis_ref, scales_ref, points_ref, skeleton_ref, ids_ref, message_ref
):
    clusters, rank, size = basis_ref.shape
    vecs = block_ref.shape[1]
    per_row = size // rank
    halves = clusters // per_row
    for half in range(halves):
        pieces = []
        for place in range(per_row):
            cluster = half * per_row + place
            vectors = block_ref[cluster].astype(jnp.bfloat16)
            message_ref[cluster * vecs : (cluster + 1) * vecs, :] = vectors
            projected = dot_nt(vectors, basis_ref[cluster])
            pieces.append(projected * scales_ref[cluster : cluster + 1, :])
        start = rows["sources"] + half * vecs
        message_ref[start : start + vecs, :] = jnp.concatenate(pieces, axis=1).astype(jnp.bfloat16)
    for axis in range(3):
        start = rows["points"] + axis * clusters
        message_ref[start : start + clusters, :] = points_ref[axis]
    lines = []
    for axis in range(3):
        skeleton = skeleton_ref[axis].astype(jnp.float32)
        for half in range(halves):
            first = half * per_row
            lines.append(
                jnp.concatenate(
                    [skeleton[first + k : first + k + 1, :] for k in range(per_row)], axis=1
                )
            )
    lines.append(jnp.zeros((rows["ids"] - rows["skeleton"] - len(lines), size), jnp.float32))
    ids = jnp.concatenate([ids_ref[0, slot] for slot in range(ids_ref.shape[1])], axis=0)
    ids = ids.astype(jnp.float32)
    lines.append(
        jnp.concatenate([ids, jnp.zeros((ids.shape[0], size - ids.shape[1]), jnp.float32)], axis=1)
    )
    lines.append(jnp.zeros((rows["end"] - rows["ids"] - ids.shape[0], size), jnp.float32))
    message_ref[rows["skeleton"] :, :] = jnp.concatenate(lines, axis=0).astype(jnp.bfloat16)


def axes_of(values, start, count):
    return [values[start + k * count : start + (k + 1) * count] for k in range(3)]


def local_kernel(
    rows, message_ref, far_ref, block_ref, prior_ref, beta_ref,
    total_ref, early_ref, left_ref, far_left_ref, counts_ref
):
    clusters, vecs, size = block_ref.shape
    blocks = counts_ref.shape[0]
    halves = far_left_ref.shape[0]
    per_row = clusters // halves
    tail = message_ref[rows["points"] :, :].astype(jnp.float32)
    axes = axes_of(tail, 0, clusters)
    left = left_rows(axes)
    right = right_rows(axes).astype(jnp.bfloat16)
    for cluster in range(clusters):
        left_ref[cluster] = left[cluster].T.astype(jnp.bfloat16)
    left_ref[clusters] = jnp.zeros_like(left_ref[clusters])
    far_left = left_rows(axes_of(tail, rows["skeleton"] - rows["points"], halves))
    for half in range(halves):
        far_left_ref[half] = far_left[half].T.astype(jnp.bfloat16)

    beta = beta_ref[...]
    sums = jnp.zeros((vecs, 2 * vecs), jnp.float32)
    for cluster in range(clusters):
        tile = tile_of(left_ref[cluster], right[cluster])
        term = dot_nt(message_ref[cluster * vecs : (cluster + 1) * vecs, :], tile)
        shift = dot_exact(beta, prior_ref[cluster])
        total_ref[cluster] = term - shift
        block = block_ref[cluster]
        sums += dot_split(block, jnp.concatenate([block, shift], axis=0))
    total_ref[clusters] = jnp.zeros_like(total_ref[clusters])
    early_ref[...] = sums

    far_ids = far_ref[...]
    lanes = lax.broadcasted_iota(jnp.int32, (clusters, blocks * per_row), 1)
    listed = jnp.zeros(lanes.shape, jnp.float32)
    for place in range(far_ref.shape[1]):
        listed += (far_ids[:, place : place + 1] == lanes).astype(jnp.float32)
    listed = listed.astype(jnp.bfloat16)
    rank = size // per_row
    rows_of = lax.broadcasted_iota(jnp.int32, (per_row, size), 0)
    widen = (lax.div(lax.broadcasted_iota(jnp.int32, (per_row, size), 1), rank) == rows_of)
    widen = widen.astype(jnp.bfloat16)
    for block in range(blocks):
        counts_ref[block] = jnp.dot(
            listed[:, block * per_row : (block + 1) * per_row], widen,
            preferred_element_type=jnp.float32,
        )


def add_kernel(rows, owner_of, pieces, last, asked_ref, *refs):
    total_in, far_in, left_ref, far_left_ref, counts_ref = refs[:5]
    count = sum(pieces)
    messages, refs = refs[5 : 5 + count], refs[5 + count :]
    if last:
        basis_ref, scales_ref, early_ref, block_ref, stacked_ref, products_ref = refs[:6]
        refs = refs[6:]
    else:
        total_out, far_out = refs[:2]
        refs = refs[2:]
    (
        total_ref, far_ref, vectors_ref, sources_ref, right_ref, far_right_ref, ids_ref,
        ids_scalar_ref, source_ref, own_ref, mirror_ref, copied,
    ) = refs
    devices = len(pieces)
    clusters = left_ref.shape[0] - 1
    size = left_ref.shape[1]
    halves, vecs, _ = far_ref.shape
    per_row = clusters // halves
    rank = size // per_row
    slots = asked_ref.shape[1]
    me = lax.axis_index("clus")
    owners = [owner_of(me, device) for device in range(devices)]

    total_ref[...] = total_in[...]
    far_ref[...] = far_in[...]
    start = 0
    for device, number in enumerate(pieces):
        first = 0
        for piece in messages[start : start + number]:
            upto = min(first + piece.shape[0], clusters * vecs)
            for row in range(first, upto, vecs):
                vectors_ref[device * clusters + row // vecs] = piece[row - first : row - first + vecs, :]
            before, first = first, first + piece.shape[0]
        rest = messages[start + number - 1]
        start += number
        offset = rows["sources"] - before
        for half in range(halves):
            sources_ref[device * halves + half] = rest[offset + half * vecs : offset + (half + 1) * vecs, :]
        tail = rest[rows["points"] - before :, :].astype(jnp.float32)
        right = right_rows(axes_of(tail, 0, clusters))
        right_ref[device * clusters : (device + 1) * clusters] = right.astype(jnp.bfloat16)
        right = right_rows(axes_of(tail, rows["skeleton"] - rows["points"], halves))
        far_right_ref[device * halves : (device + 1) * halves] = right.astype(jnp.bfloat16)
        ids = tail[rows["ids"] - rows["points"] : rows["ids"] - rows["points"] + 8]
        ids_ref[device] = ids[:, : ids_ref.shape[2]].astype(jnp.int32)
    copy = pltpu.make_async_copy(ids_ref, ids_scalar_ref, copied)
    copy.start()

    pair = 2 if devices % 2 == 0 else 1

    def far_step(turn, carry):
        terms = []
        for place in range(pair):
            device = turn * pair + place
            owner = owners[0]
            for known in range(1, devices):
                owner = jnp.where(device == known, owners[known], owner)
            for block in range(halves):
                features = far_right_ref[device * halves + block]
                sources = sources_ref[device * halves + block]
                for side in range(halves):
                    tile = values_of(far_left_ref[side], features)
                    weights = counts_ref[owner * halves + block]
                    weights = weights[side * per_row : (side + 1) * per_row]
                    tile = tile.reshape(per_row, rank, size) * weights[:, None, :]
                    tile = tile.reshape(per_row * rank, size).astype(jnp.bfloat16)
                    terms.append((side, dot_nt(sources, tile)))
        for side in range(halves):
            far_ref[side] += functools.reduce(jnp.add, [term for place, term in terms if place == side])
        return carry

    lax.fori_loop(0, devices // pair, far_step, 0)

    copy.wait()
    live = jnp.int32(0)
    for device in range(devices):
        for slot in range(slots):
            asked = asked_ref[0, slot, 0, owners[device]], asked_ref[0, slot, 1, owners[device]]
            told = ids_scalar_ref[device, 2 * slot, me], ids_scalar_ref[device, 2 * slot + 1, me]
            for row, source, own, mirror in (
                (asked[0], asked[1], asked[0], 0), (told[0], told[0], told[1], 1),
            ):
                source_ref[live] = device * clusters + source
                own_ref[live] = own
                mirror_ref[live] = mirror
                live = live + (row >= 0).astype(jnp.int32)
    for extra in range(unroll):
        source_ref[live + extra] = 0
        own_ref[live + extra] = clusters
        mirror_ref[live + extra] = 0

    def entry(place):
        source = source_ref[place]
        own = own_ref[place]
        tile = tile_of(left_ref[own], right_ref[source])
        term = dot_nt(vectors_ref[source], tile)
        rounded = term.astype(jnp.bfloat16).astype(jnp.float32)
        return own, jnp.where(mirror_ref[place] > 0, rounded, term)

    def near_step(turn, carry):
        terms = [entry(unroll * turn + place) for place in range(unroll)]
        for own, term in terms:
            total_ref[own] += term
        return carry

    lax.fori_loop(0, lax.div(live + (unroll - 1), unroll), near_step, 0)
    if not last:
        total_out[...] = total_ref[...]
        far_out[...] = far_ref[...]
        return

    sums = jnp.zeros((2 * vecs, vecs), jnp.float32)
    for cluster in range(clusters):
        side, first = cluster // per_row, (cluster % per_row) * rank
        part = far_ref[side][:, first : first + rank]
        lifted = (part * scales_ref[cluster : cluster + 1, :]).astype(jnp.bfloat16)
        shifted = total_ref[cluster] + jnp.dot(
            lifted, basis_ref[cluster], preferred_element_type=jnp.float32
        )
        stacked = jnp.concatenate([block_ref[cluster], shifted], axis=0)
        stacked_ref[cluster] = stacked
        sums += dot_split(stacked, shifted)
    early = early_ref[...]
    crossed = sums[:vecs]
    products = jnp.concatenate(
        [crossed + early[:, vecs:], crossed, sums[vecs:], early[:, :vecs]], axis=1
    )
    for part in range(products_ref.shape[0]):
        products_ref[part] = products


def finish_kernel(point_count, products_ref, stacked_ref, next_ref, alpha_ref, beta_ref):
    clusters, vecs, size = next_ref.shape
    sums = products_ref[0]
    for part in range(1, products_ref.shape[0]):
        sums = sums + products_ref[part]
    sums = sums * (1.0 / point_count)
    alpha = sums[:, :vecs]
    crossed = sums[:, vecs : 2 * vecs]
    shifted = sums[:, 2 * vecs : 3 * vecs]
    block = sums[:, 3 * vecs :]
    alpha_ref[...] = alpha
    turned = alpha.T
    crossed = dot_exact(turned, crossed - 0.5 * dot_exact(block, alpha))
    gram = shifted - crossed - crossed.T
    rows = lax.broadcasted_iota(jnp.int32, (vecs, vecs), 0)
    columns = lax.broadcasted_iota(jnp.int32, (vecs, vecs), 1)
    unit = (rows == columns).astype(jnp.float32)
    work = jnp.concatenate([gram, unit], axis=1)
    row_ids = lax.broadcasted_iota(jnp.int32, (vecs, 1), 0)
    for step in range(vecs - 1):
        pivot_row = work[step : step + 1, :]
        ratio = work[:, step : step + 1] * (1.0 / pivot_row[:, step : step + 1])
        work = work - jnp.where(row_ids > step, ratio, 0.0) * pivot_row
    pivots = jnp.sum(work[:, :vecs] * unit, axis=1, keepdims=True)
    work = work * (1.0 / jnp.sqrt(pivots))
    beta_ref[...] = jnp.where(columns >= rows, work[:, :vecs], 0.0)
    inverse = work[:, vecs:]
    joint = jnp.concatenate([-dot_exact(inverse, turned), inverse], axis=1)
    for cluster in range(clusters):
        next_ref[cluster] = dot_exact(joint, stacked_ref[cluster])


def call(kernel, out_shape, operands, scratch=(), smem=0, smem_out=0, flops=0, vmem=20 << 20):
    def specs(total, scalars):
        places = [pltpu.SMEM] * scalars + [pltpu.VMEM] * (total - scalars)
        return [pl.BlockSpec(memory_space=place) for place in places]

    return pl.pallas_call(
        kernel,
        out_shape=out_shape,
        in_specs=specs(len(operands), smem),
        out_specs=specs(len(out_shape), smem_out),
        scratch_shapes=list(scratch),
        compiler_params=pltpu.CompilerParams(vmem_limit_bytes=vmem),
        cost_estimate=pl.CostEstimate(
            flops=flops, bytes_accessed=1 << 20, transcendentals=flops // 64
        ),
    )(*operands)


def spread(message, parts):
    def passed(values, step):
        pairs = [(index, index ^ step) for index in range(parts)]
        return lax.ppermute(values, "clus", pairs)

    def group_of(steps, pieces):
        def owner_of(me, place):
            return me ^ steps[place]

        return owner_of, pieces

    if parts != 16:
        everything = lax.all_gather(message, "clus", axis=0, tiled=False)
        count = 8 if parts % 8 == 0 else 1
        yield
        for first in range(0, parts, count):
            yield (
                functools.partial(lambda first, me, place: first + place, first),
                [[everything[first + place]] for place in range(count)],
            )
        return
    core, along, inner, over = 1, 2, 4, 12
    cut = message.shape[0] // 2
    fetched = [passed(message, step) for step in (over, inner, along)]
    sibling = passed(message, core)
    token = yield
    sibling, _ = lax.optimization_barrier((sibling, token))
    token = yield group_of([0, core], [[message], [sibling]])
    fetched, _ = lax.optimization_barrier((fetched, token))
    mirrored, inward, sideways = fetched
    fetched = [
        passed(mirrored, inner), passed(mirrored, along),
        passed(sideways[:cut], inner), passed(inward[cut:], along),
    ]
    token = yield group_of(
        [over, inner, along, over ^ core, inner ^ core, along ^ core],
        [[mirrored], [inward], [sideways]]
        + [[passed(piece, core)] for piece in (mirrored, inward, sideways)],
    )
    fetched, _ = lax.optimization_barrier((fetched, token))
    mirrored_inward, mirrored_sideways, *diagonal = fetched
    fetched = [
        passed(mirrored_sideways[:cut], inner), passed(mirrored_inward[cut:], along),
    ]
    steps = [over ^ inner, over ^ along, inner ^ along]
    pieces = [[mirrored_inward], [mirrored_sideways], diagonal]
    token = yield group_of(
        steps + [step ^ core for step in steps],
        pieces + [[passed(part, core) for part in piece] for piece in pieces],
    )
    fetched, _ = lax.optimization_barrier((fetched, token))
    last = over ^ inner ^ along
    yield group_of([last, last ^ core], [fetched, [passed(part, core) for part in fetched]])


def local(
    block_vectors, prior_vectors, prior_beta, points, basis, scales, skeleton, near_pairs, far_ids
):
    clusters, vecs, size = block_vectors.shape
    rank = basis.shape[1]
    parts = lax.axis_size("clus")
    slots = near_pairs.shape[2]
    total_points = parts * clusters * size
    halves = clusters * rank // size
    rows = layout_of(clusters, vecs, rank, size)
    wide = functools.partial(jax.ShapeDtypeStruct, dtype=jnp.float32)
    narrow = functools.partial(jax.ShapeDtypeStruct, dtype=jnp.bfloat16)

    asked = near_pairs.transpose(0, 2, 3, 1)
    (message,) = call(
        functools.partial(prepare_kernel, rows),
        [narrow((rows["end"], size))],
        (
            block_vectors, basis, scales, points.transpose(1, 0, 2), skeleton.transpose(1, 0, 2),
            asked,
        ),
        vmem=56 << 20,
    )
    groups = spread(message, parts)
    next(groups)
    total, early, left, far_left, counts = call(
        functools.partial(local_kernel, rows),
        [
            wide((clusters + 1, vecs, size)),
            wide((vecs, 2 * vecs)),
            narrow((clusters + 1, size, feature_count)),
            narrow((halves, size, feature_count)),
            wide((parts * halves, clusters, size)),
        ],
        (message, far_ids, block_vectors, prior_vectors, prior_beta),
        flops=1 << 31,
    )
    far = jnp.zeros((halves, vecs, size), jnp.float32)
    lanes = -(-parts // 128) * 128
    token, seen = early, 0
    while seen < parts:
        owner_of, messages = groups.send(token)
        seen += len(messages)
        last = seen == parts
        devices = len(messages)
        entries = 2 * slots * devices + unroll
        pieces = [piece for message_pieces in messages for piece in message_pieces]
        operands = [asked, total, far, left, far_left, counts] + pieces
        out_shape = [wide((clusters + 1, vecs, size)), wide((halves, vecs, size))]
        if last:
            operands += [basis, scales, early, block_vectors]
            out_shape = [wide((clusters, 2 * vecs, size)), wide((parts, vecs, 4 * vecs))]
        total, far = call(
            functools.partial(
                add_kernel, rows, owner_of, [len(message_pieces) for message_pieces in messages], last
            ),
            out_shape,
            operands,
            scratch=[
                pltpu.VMEM((clusters + 1, vecs, size), jnp.float32),
                pltpu.VMEM((halves, vecs, size), jnp.float32),
                pltpu.VMEM((devices * clusters, vecs, size), jnp.bfloat16),
                pltpu.VMEM((devices * halves, vecs, size), jnp.bfloat16),
                pltpu.VMEM((devices * clusters, feature_count, size), jnp.bfloat16),
                pltpu.VMEM((devices * halves, feature_count, size), jnp.bfloat16),
                pltpu.VMEM((devices, 8, lanes), jnp.int32),
                pltpu.SMEM((devices, 8, lanes), jnp.int32),
                pltpu.SMEM((entries,), jnp.int32),
                pltpu.SMEM((entries,), jnp.int32),
                pltpu.SMEM((entries,), jnp.int32),
                pltpu.SemaphoreType.DMA,
            ],
            smem=1,
            flops=devices << 28,
        )
        token = far
    stacked, products = total, far
    summed = lax.all_to_all(products, "clus", split_axis=0, concat_axis=0, tiled=True)
    return tuple(
        call(
            functools.partial(finish_kernel, total_points),
            [wide((clusters, vecs, size)), wide((vecs, vecs)), wide((vecs, vecs))],
            (summed, stacked),
        )
    )


def solution(mesh):
    placed = (
        P(("group", "clus"), None, None),
        P(("group", "clus"), None, None),
        P("group", None),
        P(("group", "clus"), None, None),
        P(("group", "clus"), None, None),
        P(("group", "clus"), None),
        P(("group", "clus"), None, None),
        P(("group", "clus"), None, None, None),
        P(("group", "clus"), None),
    )
    return jax.shard_map(
        local,
        mesh=mesh,
        in_specs=placed,
        out_specs=(P(("group", "clus"), None, None), P("group", None), P("group", None)),
        check_vma=False,
    )
```

```python
import functools
import math

import jax
import jax.numpy as jnp
from jax import lax
from jax.experimental import pallas as pl
from jax.experimental.pallas import tpu as pltpu
from jax.sharding import PartitionSpec as P

root_three = 1.7320508075688772
length_scale = 0.15
scale = root_three / length_scale * math.log2(math.e)
feature_count = 16
unroll = 16
NT = (((1,), (1,)), ((), ()))


def kernel_values(squared):
    squared = jnp.maximum(squared, 1e-9)
    distance = squared * lax.rsqrt(squared)
    decay = jnp.exp2(math.log2(math.log(2.0)) - distance)
    return (distance + 1.0 / math.log(2.0)) * decay


def dot_nt(left, right):
    return lax.dot_general(left, right, NT, preferred_element_type=jnp.float32)


def dot_exact(left, right, dims=(((1,), (0,)), ((), ()))):
    return lax.dot_general(
        left, right, dims, precision=lax.Precision.HIGHEST, preferred_element_type=jnp.float32
    )


def split(values):
    high = values.astype(jnp.bfloat16)
    return high, (values - high.astype(jnp.float32)).astype(jnp.bfloat16)


def dot_split(left, right):
    left_high, left_low = split(left)
    right_high, right_low = split(right)
    return dot_nt(
        jnp.concatenate([left_high, left_high, left_low], axis=1),
        jnp.concatenate([right_high, right_low, right_high], axis=1),
    )


def values_of(left_features, right_features):
    return kernel_values(jnp.dot(left_features, right_features, preferred_element_type=jnp.float32))


def tile_of(left_features, right_features):
    return values_of(left_features, right_features).astype(jnp.bfloat16)


def pieces_of(values):
    high = values.astype(jnp.bfloat16).astype(jnp.float32)
    rest = values - high
    middle = rest.astype(jnp.bfloat16).astype(jnp.float32)
    return [high, middle, rest - middle]


def norm_pieces(axes):
    norm = axes[0] * axes[0] + axes[1] * axes[1] + axes[2] * axes[2]
    return pieces_of(norm * (scale * scale))


def stack_rows(rows):
    rows = rows + [jnp.zeros_like(rows[0])] * (feature_count - len(rows))
    return jnp.transpose(jnp.stack(rows, axis=0), (1, 0, 2))


def left_rows(axes):
    one = jnp.ones_like(axes[0])
    return stack_rows([axis for axis in axes for _ in range(3)] + norm_pieces(axes) + [one] * 3)


def right_rows(axes):
    one = jnp.ones_like(axes[0])
    crossed = [piece for axis in axes for piece in pieces_of(axis * (-2.0 * scale * scale))]
    return stack_rows(crossed + [one] * 3 + norm_pieces(axes))


def layout_of(clusters, vecs, rank, size):
    halves = clusters * rank // size
    rows = {"sources": clusters * vecs}
    rows["points"] = rows["sources"] + halves * vecs
    rows["skeleton"] = rows["points"] + 3 * clusters
    rows["ids"] = -(-(rows["skeleton"] + 3 * halves) // 8) * 8
    rows["end"] = -(-(rows["ids"] + 8) // 16) * 16
    return rows


def prepare_kernel(
    rows, block_ref, basis_ref, scales_ref, points_ref, skeleton_ref, ids_ref, message_ref
):
    clusters, rank, size = basis_ref.shape
    vecs = block_ref.shape[1]
    per_row = size // rank
    halves = clusters // per_row
    for half in range(halves):
        pieces = []
        for place in range(per_row):
            cluster = half * per_row + place
            vectors = block_ref[cluster].astype(jnp.bfloat16)
            message_ref[cluster * vecs : (cluster + 1) * vecs, :] = vectors
            projected = dot_nt(vectors, basis_ref[cluster])
            pieces.append(projected * scales_ref[cluster : cluster + 1, :])
        start = rows["sources"] + half * vecs
        message_ref[start : start + vecs, :] = jnp.concatenate(pieces, axis=1).astype(jnp.bfloat16)
    for axis in range(3):
        start = rows["points"] + axis * clusters
        message_ref[start : start + clusters, :] = points_ref[axis]
    lines = []
    for axis in range(3):
        skeleton = skeleton_ref[axis].astype(jnp.float32)
        for half in range(halves):
            first = half * per_row
            lines.append(
                jnp.concatenate(
                    [skeleton[first + k : first + k + 1, :] for k in range(per_row)], axis=1
                )
            )
    lines.append(jnp.zeros((rows["ids"] - rows["skeleton"] - len(lines), size), jnp.float32))
    ids = jnp.concatenate([ids_ref[0, slot] for slot in range(ids_ref.shape[1])], axis=0)
    ids = ids.astype(jnp.float32)
    lines.append(
        jnp.concatenate([ids, jnp.zeros((ids.shape[0], size - ids.shape[1]), jnp.float32)], axis=1)
    )
    lines.append(jnp.zeros((rows["end"] - rows["ids"] - ids.shape[0], size), jnp.float32))
    message_ref[rows["skeleton"] :, :] = jnp.concatenate(lines, axis=0).astype(jnp.bfloat16)


def axes_of(values, start, count):
    return [values[start + k * count : start + (k + 1) * count] for k in range(3)]


def local_kernel(
    rows, message_ref, far_ref, block_ref, prior_ref, beta_ref,
    total_ref, early_ref, left_ref, far_left_ref, counts_ref
):
    clusters, vecs, size = block_ref.shape
    blocks = counts_ref.shape[0]
    halves = far_left_ref.shape[0]
    per_row = clusters // halves
    tail = message_ref[rows["points"] :, :].astype(jnp.float32)
    axes = axes_of(tail, 0, clusters)
    left = left_rows(axes)
    right = right_rows(axes).astype(jnp.bfloat16)
    for cluster in range(clusters):
        left_ref[cluster] = left[cluster].T.astype(jnp.bfloat16)
    left_ref[clusters] = jnp.zeros_like(left_ref[clusters])
    far_left = left_rows(axes_of(tail, rows["skeleton"] - rows["points"], halves))
    for half in range(halves):
        far_left_ref[half] = far_left[half].T.astype(jnp.bfloat16)

    beta = beta_ref[...]
    sums = jnp.zeros((vecs, 2 * vecs), jnp.float32)
    for cluster in range(clusters):
        tile = tile_of(left_ref[cluster], right[cluster])
        term = dot_nt(message_ref[cluster * vecs : (cluster + 1) * vecs, :], tile)
        shift = dot_exact(beta, prior_ref[cluster])
        total_ref[cluster] = term - shift
        block = block_ref[cluster]
        sums += dot_split(block, jnp.concatenate([block, shift], axis=0))
    total_ref[clusters] = jnp.zeros_like(total_ref[clusters])
    early_ref[...] = sums

    far_ids = far_ref[...]
    lanes = lax.broadcasted_iota(jnp.int32, (clusters, blocks * per_row), 1)
    listed = jnp.zeros(lanes.shape, jnp.float32)
    for place in range(far_ref.shape[1]):
        listed += (far_ids[:, place : place + 1] == lanes).astype(jnp.float32)
    listed = listed.astype(jnp.bfloat16)
    rank = size // per_row
    rows_of = lax.broadcasted_iota(jnp.int32, (per_row, size), 0)
    widen = (lax.div(lax.broadcasted_iota(jnp.int32, (per_row, size), 1), rank) == rows_of)
    widen = widen.astype(jnp.bfloat16)
    for block in range(blocks):
        counts_ref[block] = jnp.dot(
            listed[:, block * per_row : (block + 1) * per_row], widen,
            preferred_element_type=jnp.float32,
        )


def add_kernel(rows, owner_of, pieces, last, asked_ref, *refs):
    total_in, far_in, left_ref, far_left_ref, counts_ref = refs[:5]
    count = sum(pieces)
    messages, refs = refs[5 : 5 + count], refs[5 + count :]
    if last:
        basis_ref, scales_ref, early_ref, block_ref, stacked_ref, products_ref = refs[:6]
        refs = refs[6:]
    else:
        total_out, far_out = refs[:2]
        refs = refs[2:]
    (
        total_ref, far_ref, vectors_ref, sources_ref, right_ref, far_right_ref, ids_ref,
        ids_scalar_ref, source_ref, own_ref, mirror_ref, copied,
    ) = refs
    devices = len(pieces)
    clusters = left_ref.shape[0] - 1
    size = left_ref.shape[1]
    halves, vecs, _ = far_ref.shape
    per_row = clusters // halves
    rank = size // per_row
    slots = asked_ref.shape[1]
    me = lax.axis_index("clus")
    owners = [owner_of(me, device) for device in range(devices)]

    total_ref[...] = total_in[...]
    far_ref[...] = far_in[...]
    start = 0
    for device, number in enumerate(pieces):
        first = 0
        for piece in messages[start : start + number]:
            upto = min(first + piece.shape[0], clusters * vecs)
            for row in range(first, upto, vecs):
                vectors_ref[device * clusters + row // vecs] = piece[row - first : row - first + vecs, :]
            before, first = first, first + piece.shape[0]
        rest = messages[start + number - 1]
        start += number
        offset = rows["sources"] - before
        for half in range(halves):
            sources_ref[device * halves + half] = rest[offset + half * vecs : offset + (half + 1) * vecs, :]
        tail = rest[rows["points"] - before :, :].astype(jnp.float32)
        right = right_rows(axes_of(tail, 0, clusters))
        right_ref[device * clusters : (device + 1) * clusters] = right.astype(jnp.bfloat16)
        right = right_rows(axes_of(tail, rows["skeleton"] - rows["points"], halves))
        far_right_ref[device * halves : (device + 1) * halves] = right.astype(jnp.bfloat16)
        ids = tail[rows["ids"] - rows["points"] : rows["ids"] - rows["points"] + 8]
        ids_ref[device] = ids[:, : ids_ref.shape[2]].astype(jnp.int32)
    copy = pltpu.make_async_copy(ids_ref, ids_scalar_ref, copied)
    copy.start()

    pair = devices // 2 if devices % 2 == 0 else 1

    def far_step(turn, carry):
        terms = []
        for place in range(pair):
            device = turn * pair + place
            owner = owners[0]
            for known in range(1, devices):
                owner = jnp.where(device == known, owners[known], owner)
            for block in range(halves):
                features = far_right_ref[device * halves + block]
                sources = sources_ref[device * halves + block]
                for side in range(halves):
                    tile = values_of(far_left_ref[side], features)
                    weights = counts_ref[owner * halves + block]
                    weights = weights[side * per_row : (side + 1) * per_row]
                    tile = tile.reshape(per_row, rank, size) * weights[:, None, :]
                    tile = tile.reshape(per_row * rank, size).astype(jnp.bfloat16)
                    terms.append((side, dot_nt(sources, tile)))
        for side, term in terms:
            far_ref[side] += term
        return carry

    lax.fori_loop(0, devices // pair, far_step, 0)

    copy.wait()
    live = jnp.int32(0)
    for device in range(devices):
        for slot in range(slots):
            asked = asked_ref[0, slot, 0, owners[device]], asked_ref[0, slot, 1, owners[device]]
            told = ids_scalar_ref[device, 2 * slot, me], ids_scalar_ref[device, 2 * slot + 1, me]
            for row, source, own, mirror in (
                (asked[0], asked[1], asked[0], 0), (told[0], told[0], told[1], 1),
            ):
                source_ref[live] = device * clusters + source
                own_ref[live] = own
                mirror_ref[live] = mirror
                live = live + (row >= 0).astype(jnp.int32)
    for extra in range(unroll):
        source_ref[live + extra] = 0
        own_ref[live + extra] = clusters
        mirror_ref[live + extra] = 0

    def entry(place):
        source = source_ref[place]
        own = own_ref[place]
        tile = tile_of(left_ref[own], right_ref[source])
        term = dot_nt(vectors_ref[source], tile)
        rounded = term.astype(jnp.bfloat16).astype(jnp.float32)
        return own, jnp.where(mirror_ref[place] > 0, rounded, term)

    def near_step(first, together):
        terms = [entry(first + place) for place in range(together)]
        for own, term in terms:
            total_ref[own] += term

    half, few = unroll // 2, unroll // 4
    turns = lax.div(live + (few - 1), unroll)

    def full_step(turn, carry):
        near_step(unroll * turn, unroll)
        return carry

    lax.fori_loop(0, turns, full_step, 0)
    done = unroll * turns
    more = live - done > few

    @pl.when(more)
    def _():
        near_step(done, half)

    done = done + jnp.where(more, half, 0)

    @pl.when(live > done)
    def _():
        near_step(done, few)

    if not last:
        total_out[...] = total_ref[...]
        far_out[...] = far_ref[...]
        return

    sums = jnp.zeros((2 * vecs, vecs), jnp.float32)
    place_ids = lax.broadcasted_iota(jnp.int32, (per_row, vecs, size), 0)
    lane_ids = lax.broadcasted_iota(jnp.int32, (per_row, vecs, size), 2)
    own_lanes = lax.div(lane_ids, rank) == place_ids
    for side in range(halves):
        scales = scales_ref[side * per_row : (side + 1) * per_row, :]
        scales = jnp.concatenate([scales[place : place + 1] for place in range(per_row)], axis=1)
        lifted = jnp.where(own_lanes, (far_ref[side] * scales)[None], 0.0)
        lifted = lifted.reshape(per_row * vecs, size).astype(jnp.bfloat16)
        basis = basis_ref[side * per_row : (side + 1) * per_row].reshape(per_row * rank, size)
        terms = jnp.dot(lifted, basis, preferred_element_type=jnp.float32)
        for place in range(per_row):
            cluster = side * per_row + place
            shifted = total_ref[cluster] + terms[place * vecs : (place + 1) * vecs]
            stacked = jnp.concatenate([block_ref[cluster], shifted], axis=0)
            stacked_ref[cluster] = stacked
            sums += dot_split(stacked, shifted)
    early = early_ref[...]
    crossed = sums[:vecs]
    products = jnp.concatenate(
        [crossed + early[:, vecs:], crossed, sums[vecs:], early[:, :vecs]], axis=1
    )
    for part in range(products_ref.shape[0]):
        products_ref[part] = products


def finish_kernel(point_count, products_ref, stacked_ref, next_ref, alpha_ref, beta_ref):
    clusters, vecs, size = next_ref.shape
    sums = products_ref[0]
    for part in range(1, products_ref.shape[0]):
        sums = sums + products_ref[part]
    sums = sums * (1.0 / point_count)
    alpha = sums[:, :vecs]
    crossed = sums[:, vecs : 2 * vecs]
    shifted = sums[:, 2 * vecs : 3 * vecs]
    block = sums[:, 3 * vecs :]
    alpha_ref[...] = alpha
    turned = alpha.T
    crossed = dot_exact(turned, crossed - 0.5 * dot_exact(block, alpha))
    gram = shifted - crossed - crossed.T
    rows = lax.broadcasted_iota(jnp.int32, (vecs, vecs), 0)
    columns = lax.broadcasted_iota(jnp.int32, (vecs, vecs), 1)
    unit = (rows == columns).astype(jnp.float32)
    work = jnp.concatenate([gram, unit], axis=1)
    row_ids = lax.broadcasted_iota(jnp.int32, (vecs, 1), 0)
    full = (vecs, 2 * vecs)
    row_full = lax.broadcasted_iota(jnp.int32, full, 0)
    for step in range(0, vecs - 2, 2):
        left = jnp.broadcast_to(work[:, step : step + 1], full)
        right = jnp.broadcast_to(work[:, step + 1 : step + 2], full)
        first, second = work[step : step + 1, :], work[step + 1 : step + 2, :]
        corner, side = left[step : step + 1, :], left[step + 1 : step + 2, :]
        other = right[step + 1 : step + 2, :]
        scale = 1.0 / (corner * other - side * side)
        first, second = (other * first - side * second) * scale, (corner * second - side * first) * scale
        below = row_full > step + 1
        work = work - jnp.where(below, left * first + right * second, 0.0)
    pivots = jnp.sum(work[:, :vecs] * unit, axis=1, keepdims=True)
    beside = (columns == rows + 1).astype(jnp.float32)
    ratios = jnp.sum(work[:, :vecs] * beside, axis=1, keepdims=True) / pivots
    taken = jnp.where(row_ids % 2 == 0, ratios, 0.0) * work
    work = work - jnp.concatenate([jnp.zeros((1, 2 * vecs), jnp.float32), taken[:-1]], axis=0)
    pivots = jnp.sum(work[:, :vecs] * unit, axis=1, keepdims=True)
    work = work * (1.0 / jnp.sqrt(pivots))
    beta_ref[...] = jnp.where(columns >= rows, work[:, :vecs], 0.0)
    inverse = work[:, vecs:]
    joint = jnp.concatenate([-dot_exact(inverse, turned), inverse], axis=1)
    for cluster in range(clusters):
        next_ref[cluster] = dot_exact(joint, stacked_ref[cluster])


def call(kernel, out_shape, operands, scratch=(), smem=0, smem_out=0, flops=0, vmem=20 << 20):
    def specs(total, scalars):
        places = [pltpu.SMEM] * scalars + [pltpu.VMEM] * (total - scalars)
        return [pl.BlockSpec(memory_space=place) for place in places]

    return pl.pallas_call(
        kernel,
        out_shape=out_shape,
        in_specs=specs(len(operands), smem),
        out_specs=specs(len(out_shape), smem_out),
        scratch_shapes=list(scratch),
        compiler_params=pltpu.CompilerParams(vmem_limit_bytes=vmem),
        cost_estimate=pl.CostEstimate(
            flops=flops, bytes_accessed=1 << 20, transcendentals=flops // 64
        ),
    )(*operands)


def spread(message, parts):
    def passed(values, step):
        pairs = [(index, index ^ step) for index in range(parts)]
        return lax.ppermute(values, "clus", pairs)

    def group_of(steps, pieces):
        def owner_of(me, place):
            return me ^ steps[place]

        return owner_of, pieces

    if parts != 16:
        everything = lax.all_gather(message, "clus", axis=0, tiled=False)
        count = 8 if parts % 8 == 0 else 1
        yield
        for first in range(0, parts, count):
            yield (
                functools.partial(lambda first, me, place: first + place, first),
                [[everything[first + place]] for place in range(count)],
            )
        return
    core, along, inner, over = 1, 2, 4, 12
    cut = message.shape[0] // 2
    fetched = [passed(message, step) for step in (over, inner, along)]
    sibling = passed(message, core)
    token = yield
    sibling, _ = lax.optimization_barrier((sibling, token))
    token = yield group_of([0, core], [[message], [sibling]])
    fetched, _ = lax.optimization_barrier((fetched, token))
    mirrored, inward, sideways = fetched
    fetched = [
        passed(mirrored, inner), passed(mirrored, along),
        passed(sideways[:cut], inner), passed(inward[cut:], along),
    ]
    token = yield group_of(
        [over, inner, along, over ^ core, inner ^ core, along ^ core],
        [[mirrored], [inward], [sideways]]
        + [[passed(piece, core)] for piece in (mirrored, inward, sideways)],
    )
    fetched, _ = lax.optimization_barrier((fetched, token))
    mirrored_inward, mirrored_sideways, *diagonal = fetched
    fetched = [
        passed(mirrored_sideways[:cut], inner), passed(mirrored_inward[cut:], along),
    ]
    steps = [over ^ inner, over ^ along, inner ^ along]
    pieces = [[mirrored_inward], [mirrored_sideways], diagonal]
    token = yield group_of(
        steps + [step ^ core for step in steps],
        pieces + [[passed(part, core) for part in piece] for piece in pieces],
    )
    fetched, _ = lax.optimization_barrier((fetched, token))
    last = over ^ inner ^ along
    yield group_of([last, last ^ core], [fetched, [passed(part, core) for part in fetched]])


def local(
    block_vectors, prior_vectors, prior_beta, points, basis, scales, skeleton, near_pairs, far_ids
):
    clusters, vecs, size = block_vectors.shape
    rank = basis.shape[1]
    parts = lax.axis_size("clus")
    slots = near_pairs.shape[2]
    total_points = parts * clusters * size
    halves = clusters * rank // size
    rows = layout_of(clusters, vecs, rank, size)
    wide = functools.partial(jax.ShapeDtypeStruct, dtype=jnp.float32)
    narrow = functools.partial(jax.ShapeDtypeStruct, dtype=jnp.bfloat16)

    asked = near_pairs.transpose(0, 2, 3, 1)
    (message,) = call(
        functools.partial(prepare_kernel, rows),
        [narrow((rows["end"], size))],
        (
            block_vectors, basis, scales, points.transpose(1, 0, 2), skeleton.transpose(1, 0, 2),
            asked,
        ),
        vmem=56 << 20,
    )
    groups = spread(message, parts)
    next(groups)
    total, early, left, far_left, counts = call(
        functools.partial(local_kernel, rows),
        [
            wide((clusters + 1, vecs, size)),
            wide((vecs, 2 * vecs)),
            narrow((clusters + 1, size, feature_count)),
            narrow((halves, size, feature_count)),
            wide((parts * halves, clusters, size)),
        ],
        (message, far_ids, block_vectors, prior_vectors, prior_beta),
        flops=1 << 31,
    )
    far = jnp.zeros((halves, vecs, size), jnp.float32)
    lanes = -(-parts // 128) * 128
    token, seen = early, 0
    while seen < parts:
        owner_of, messages = groups.send(token)
        seen += len(messages)
        last = seen == parts
        devices = len(messages)
        entries = 2 * slots * devices + unroll
        pieces = [piece for message_pieces in messages for piece in message_pieces]
        operands = [asked, total, far, left, far_left, counts] + pieces
        out_shape = [wide((clusters + 1, vecs, size)), wide((halves, vecs, size))]
        if last:
            operands += [basis, scales, early, block_vectors]
            out_shape = [wide((clusters, 2 * vecs, size)), wide((parts, vecs, 4 * vecs))]
        total, far = call(
            functools.partial(
                add_kernel, rows, owner_of, [len(message_pieces) for message_pieces in messages], last
            ),
            out_shape,
            operands,
            scratch=[
                pltpu.VMEM((clusters + 1, vecs, size), jnp.float32),
                pltpu.VMEM((halves, vecs, size), jnp.float32),
                pltpu.VMEM((devices * clusters, vecs, size), jnp.bfloat16),
                pltpu.VMEM((devices * halves, vecs, size), jnp.bfloat16),
                pltpu.VMEM((devices * clusters, feature_count, size), jnp.bfloat16),
                pltpu.VMEM((devices * halves, feature_count, size), jnp.bfloat16),
                pltpu.VMEM((devices, 8, lanes), jnp.int32),
                pltpu.SMEM((devices, 8, lanes), jnp.int32),
                pltpu.SMEM((entries,), jnp.int32),
                pltpu.SMEM((entries,), jnp.int32),
                pltpu.SMEM((entries,), jnp.int32),
                pltpu.SemaphoreType.DMA,
            ],
            smem=1,
            flops=devices << 28,
        )
        token = far
    stacked, products = total, far
    summed = lax.all_to_all(products, "clus", split_axis=0, concat_axis=0, tiled=True)
    return tuple(
        call(
            functools.partial(finish_kernel, total_points),
            [wide((clusters, vecs, size)), wide((vecs, vecs)), wide((vecs, vecs))],
            (summed, stacked),
        )
    )


def solution(mesh):
    placed = (
        P(("group", "clus"), None, None),
        P(("group", "clus"), None, None),
        P("group", None),
        P(("group", "clus"), None, None),
        P(("group", "clus"), None, None),
        P(("group", "clus"), None),
        P(("group", "clus"), None, None),
        P(("group", "clus"), None, None, None),
        P(("group", "clus"), None),
    )
    return jax.shard_map(
        local,
        mesh=mesh,
        in_specs=placed,
        out_specs=(P(("group", "clus"), None, None), P("group", None), P("group", None)),
        check_vma=False,
    )
```

```python
import functools
import math

import jax
import jax.numpy as jnp
from jax import lax
from jax.experimental import pallas as pl
from jax.experimental.pallas import tpu as pltpu
from jax.sharding import PartitionSpec as P

root_three = 1.7320508075688772
length_scale = 0.15
scale = root_three / length_scale * math.log2(math.e)
feature_count = 16
unroll = 16
NT = (((1,), (1,)), ((), ()))


def kernel_values(squared):
    squared = jnp.maximum(squared, 1e-9)
    distance = squared * lax.rsqrt(squared)
    decay = jnp.exp2(math.log2(math.log(2.0)) - distance)
    return (distance + 1.0 / math.log(2.0)) * decay


def dot_nt(left, right):
    return lax.dot_general(left, right, NT, preferred_element_type=jnp.float32)


def dot_exact(left, right, dims=(((1,), (0,)), ((), ()))):
    return lax.dot_general(
        left, right, dims, precision=lax.Precision.HIGHEST, preferred_element_type=jnp.float32
    )


def split(values):
    high = values.astype(jnp.bfloat16)
    return high, (values - high.astype(jnp.float32)).astype(jnp.bfloat16)


def dot_split(left, right):
    left_high, left_low = split(left)
    right_high, right_low = split(right)
    return dot_nt(
        jnp.concatenate([left_high, left_high, left_low], axis=1),
        jnp.concatenate([right_high, right_low, right_high], axis=1),
    )


def values_of(left_features, right_features):
    return kernel_values(jnp.dot(left_features, right_features, preferred_element_type=jnp.float32))


def tile_of(left_features, right_features):
    return values_of(left_features, right_features).astype(jnp.bfloat16)


def pieces_of(values):
    high = values.astype(jnp.bfloat16).astype(jnp.float32)
    rest = values - high
    middle = rest.astype(jnp.bfloat16).astype(jnp.float32)
    return [high, middle, rest - middle]


def norm_pieces(axes):
    norm = axes[0] * axes[0] + axes[1] * axes[1] + axes[2] * axes[2]
    return pieces_of(norm * (scale * scale))


def stack_rows(rows):
    rows = rows + [jnp.zeros_like(rows[0])] * (feature_count - len(rows))
    return jnp.transpose(jnp.stack(rows, axis=0), (1, 0, 2))


def left_rows(axes):
    one = jnp.ones_like(axes[0])
    return stack_rows([axis for axis in axes for _ in range(3)] + norm_pieces(axes) + [one] * 3)


def right_rows(axes):
    one = jnp.ones_like(axes[0])
    crossed = [piece for axis in axes for piece in pieces_of(axis * (-2.0 * scale * scale))]
    return stack_rows(crossed + [one] * 3 + norm_pieces(axes))


def layout_of(clusters, vecs, rank, size):
    halves = clusters * rank // size
    rows = {"sources": clusters * vecs}
    rows["points"] = rows["sources"] + halves * vecs
    rows["skeleton"] = rows["points"] + 3 * clusters
    rows["ids"] = -(-(rows["skeleton"] + 3 * halves) // 8) * 8
    rows["end"] = -(-(rows["ids"] + 8) // 16) * 16
    return rows


def prepare_kernel(
    rows, block_ref, basis_ref, scales_ref, points_ref, skeleton_ref, ids_ref, message_ref, *half_refs
):
    clusters, rank, size = basis_ref.shape
    vecs = block_ref.shape[1]
    per_row = size // rank
    halves = clusters // per_row
    for half in range(halves):
        pieces = []
        for place in range(per_row):
            cluster = half * per_row + place
            vectors = block_ref[cluster].astype(jnp.bfloat16)
            message_ref[cluster * vecs : (cluster + 1) * vecs, :] = vectors
            projected = dot_nt(vectors, basis_ref[cluster])
            pieces.append(projected * scales_ref[cluster : cluster + 1, :])
        start = rows["sources"] + half * vecs
        message_ref[start : start + vecs, :] = jnp.concatenate(pieces, axis=1).astype(jnp.bfloat16)
    for axis in range(3):
        start = rows["points"] + axis * clusters
        message_ref[start : start + clusters, :] = points_ref[axis]
    lines = []
    for axis in range(3):
        skeleton = skeleton_ref[axis].astype(jnp.float32)
        for half in range(halves):
            first = half * per_row
            lines.append(
                jnp.concatenate(
                    [skeleton[first + k : first + k + 1, :] for k in range(per_row)], axis=1
                )
            )
    lines.append(jnp.zeros((rows["ids"] - rows["skeleton"] - len(lines), size), jnp.float32))
    ids = jnp.concatenate([ids_ref[0, slot] for slot in range(ids_ref.shape[1])], axis=0)
    ids = ids.astype(jnp.float32)
    lines.append(
        jnp.concatenate([ids, jnp.zeros((ids.shape[0], size - ids.shape[1]), jnp.float32)], axis=1)
    )
    lines.append(jnp.zeros((rows["end"] - rows["ids"] - ids.shape[0], size), jnp.float32))
    message_ref[rows["skeleton"] :, :] = jnp.concatenate(lines, axis=0).astype(jnp.bfloat16)
    for place, half_ref in enumerate(half_refs):
        count = half_ref.shape[0]
        half_ref[...] = message_ref[place * count : (place + 1) * count, :]


def axes_of(values, start, count):
    return [values[start + k * count : start + (k + 1) * count] for k in range(3)]


def local_kernel(rows, targets, *refs):
    messages, far_refs, refs = refs[:targets], refs[targets : 2 * targets], refs[2 * targets :]
    (
        block_ref, prior_ref, beta_ref,
        total_ref, far_ref, early_ref, left_ref, far_left_ref, counts_ref, ids_ref,
    ) = refs
    clusters, vecs, size = block_ref.shape
    blocks = counts_ref.shape[0] // targets
    halves = far_left_ref.shape[0] // targets
    per_row = clusters // halves
    rank = size // per_row
    lanes = lax.broadcasted_iota(jnp.int32, (clusters, blocks * per_row), 1)
    row_ids = lax.broadcasted_iota(jnp.int32, (per_row, size), 0)
    widen = lax.div(lax.broadcasted_iota(jnp.int32, (per_row, size), 1), rank) == row_ids
    widen = widen.astype(jnp.bfloat16)
    for target in range(targets):
        tail = messages[target][rows["points"] :, :].astype(jnp.float32)
        axes = axes_of(tail, 0, clusters)
        left = left_rows(axes)
        for cluster in range(clusters):
            left_ref[target * clusters + cluster] = left[cluster].T.astype(jnp.bfloat16)
        if target == 0:
            right = right_rows(axes).astype(jnp.bfloat16)
        far_left = left_rows(axes_of(tail, rows["skeleton"] - rows["points"], halves))
        for half in range(halves):
            far_left_ref[target * halves + half] = far_left[half].T.astype(jnp.bfloat16)
        ids = tail[rows["ids"] - rows["points"] : rows["ids"] - rows["points"] + 8]
        ids_ref[target] = ids[:, : ids_ref.shape[2]].astype(jnp.int32)

        far_ids = far_refs[target][...]
        listed = jnp.zeros(lanes.shape, jnp.float32)
        for place in range(far_ids.shape[1]):
            listed += (far_ids[:, place : place + 1] == lanes).astype(jnp.float32)
        listed = listed.astype(jnp.bfloat16)
        for block in range(blocks):
            counts_ref[target * blocks + block] = jnp.dot(
                listed[:, block * per_row : (block + 1) * per_row], widen,
                preferred_element_type=jnp.float32,
            )

    beta = beta_ref[...]
    sums = jnp.zeros((vecs, 2 * vecs), jnp.float32)
    for cluster in range(clusters):
        tile = tile_of(left_ref[cluster], right[cluster])
        term = dot_nt(messages[0][cluster * vecs : (cluster + 1) * vecs, :], tile)
        shift = dot_exact(beta, prior_ref[cluster])
        total_ref[cluster] = term - shift
        block = block_ref[cluster]
        sums += dot_split(block, jnp.concatenate([block, shift], axis=0))
    early_ref[...] = sums
    total_ref[clusters:] = jnp.zeros((total_ref.shape[0] - clusters, vecs, size), jnp.float32)
    far_ref[...] = jnp.zeros_like(far_ref)


def add_kernel(rows, owner_of, target_of, pieces, last, *refs):
    total_in, far_in, left_ref, far_left_ref, counts_ref, own_ids_ref = refs[:6]
    count = sum(pieces)
    messages, refs = refs[6 : 6 + count], refs[6 + count :]
    outputs, refs = refs[: 3 if last else 2], refs[3 if last else 2 :]
    (
        total_ref, far_ref, vectors_ref, sources_ref, right_ref, far_right_ref, ids_ref,
        ids_scalar_ref, source_ref, own_ref, mirror_ref, copied,
    ) = refs
    devices = len(pieces)
    targets = own_ids_ref.shape[0]
    clusters = left_ref.shape[0] // targets
    size = left_ref.shape[1]
    sides = far_ref.shape[0]
    halves = sides // targets
    vecs = far_ref.shape[1]
    per_row = clusters // halves
    rank = size // per_row
    slots = rows["slots"]
    blocks = counts_ref.shape[0] // targets
    me = lax.axis_index("clus")
    owners = [owner_of(me, device) for device in range(devices)]

    total_ref[...] = total_in[...]
    far_ref[...] = far_in[...]
    start = 0
    for device, number in enumerate(pieces):
        first = 0
        for piece in messages[start : start + number]:
            upto = min(first + piece.shape[0], clusters * vecs)
            for row in range(first, upto, vecs):
                vectors_ref[device * clusters + row // vecs] = piece[row - first : row - first + vecs, :]
            before, first = first, first + piece.shape[0]
        rest = messages[start + number - 1]
        start += number
        offset = rows["sources"] - before
        for half in range(halves):
            sources_ref[device * halves + half] = rest[offset + half * vecs : offset + (half + 1) * vecs, :]
        tail = rest[rows["points"] - before :, :].astype(jnp.float32)
        right = right_rows(axes_of(tail, 0, clusters))
        right_ref[device * clusters : (device + 1) * clusters] = right.astype(jnp.bfloat16)
        right = right_rows(axes_of(tail, rows["skeleton"] - rows["points"], halves))
        far_right_ref[device * halves : (device + 1) * halves] = right.astype(jnp.bfloat16)
        ids = tail[rows["ids"] - rows["points"] : rows["ids"] - rows["points"] + 8]
        ids_ref[device] = ids[:, : ids_ref.shape[2]].astype(jnp.int32)
    for target in range(targets):
        ids_ref[devices + target] = own_ids_ref[target]
    copy = pltpu.make_async_copy(ids_ref, ids_scalar_ref, copied)
    copy.start()

    pair = 2 if devices % 2 == 0 else 1

    def far_step(turn, carry):
        terms = []
        for place in range(pair):
            device = turn * pair + place
            owner = owners[0]
            for known in range(1, devices):
                owner = jnp.where(device == known, owners[known], owner)
            for block in range(halves):
                features = far_right_ref[device * halves + block]
                sources = sources_ref[device * halves + block]
                for side in range(sides):
                    tile = values_of(far_left_ref[side], features)
                    weights = counts_ref[(side // halves) * blocks + owner * halves + block]
                    first = (side % halves) * per_row
                    weights = weights[first : first + per_row]
                    tile = tile.reshape(per_row, rank, size) * weights[:, None, :]
                    tile = tile.reshape(per_row * rank, size).astype(jnp.bfloat16)
                    terms.append((side, dot_nt(sources, tile)))
        for side, term in terms:
            far_ref[side] += term
        return carry

    lax.fori_loop(0, devices // pair, far_step, 0)

    copy.wait()
    live = jnp.int32(0)
    for device in range(devices):
        for target in range(targets):
            asker = target_of(me, target)
            base = target * clusters
            for slot in range(slots):
                row, partner = 2 * slot, 2 * slot + 1
                asked = [ids_scalar_ref[devices + target, k, owners[device]] for k in (row, partner)]
                told = [ids_scalar_ref[device, k, asker] for k in (row, partner)]
                for alive, source, own, mirror in (
                    (asked[0], asked[1], asked[0], 0), (told[0], told[0], told[1], 1),
                ):
                    source_ref[live] = device * clusters + source
                    own_ref[live] = base + own
                    mirror_ref[live] = mirror
                    live = live + (alive >= 0).astype(jnp.int32)
    for extra in range(unroll):
        source_ref[live + extra] = 0
        own_ref[live + extra] = targets * clusters
        mirror_ref[live + extra] = 0

    def entry(place):
        source = source_ref[place]
        own = own_ref[place]
        tile = tile_of(left_ref[jnp.minimum(own, targets * clusters - 1)], right_ref[source])
        term = dot_nt(vectors_ref[source], tile)
        rounded = term.astype(jnp.bfloat16).astype(jnp.float32)
        return own, jnp.where(mirror_ref[place] > 0, rounded, term)

    def near_step(first, together):
        terms = [entry(first + place) for place in range(together)]
        for own, term in terms:
            total_ref[own] += term

    half, few = unroll // 2, unroll // 4
    turns = lax.div(live + (few - 1), unroll)

    def full_step(turn, carry):
        near_step(unroll * turn, unroll)
        return carry

    lax.fori_loop(0, turns, full_step, 0)
    done = unroll * turns
    more = live - done > few

    @pl.when(more)
    def _():
        near_step(done, half)

    done = done + jnp.where(more, half, 0)

    @pl.when(live > done)
    def _():
        near_step(done, few)

    if not last:
        outputs[0][...] = total_ref[...]
        outputs[1][...] = far_ref[...]
        return
    outputs[0][...] = total_ref[:clusters]
    outputs[1][...] = far_ref[:halves]
    outputs[2][:clusters] = total_ref[(targets - 1) * clusters : targets * clusters]
    outputs[2][clusters:] = far_ref[(targets - 1) * halves :]


def combine_kernel(
    given, total_ref, far_ref, given_ref, basis_ref, scales_ref, early_ref, block_ref,
    stacked_ref, products_ref
):
    clusters, vecs, size = total_ref.shape
    halves = far_ref.shape[0]
    per_row = clusters // halves
    rank = size // per_row
    sums = jnp.zeros((2 * vecs, vecs), jnp.float32)
    place_ids = lax.broadcasted_iota(jnp.int32, (per_row, vecs, size), 0)
    lane_ids = lax.broadcasted_iota(jnp.int32, (per_row, vecs, size), 2)
    own_lanes = lax.div(lane_ids, rank) == place_ids
    for side in range(halves):
        scales = scales_ref[side * per_row : (side + 1) * per_row, :]
        scales = jnp.concatenate([scales[place : place + 1] for place in range(per_row)], axis=1)
        gathered = far_ref[side]
        if given:
            gathered = gathered + given_ref[clusters + side]
        lifted = jnp.where(own_lanes, (gathered * scales)[None], 0.0)
        lifted = lifted.reshape(per_row * vecs, size).astype(jnp.bfloat16)
        basis = basis_ref[side * per_row : (side + 1) * per_row].reshape(per_row * rank, size)
        terms = jnp.dot(lifted, basis, preferred_element_type=jnp.float32)
        for place in range(per_row):
            cluster = side * per_row + place
            shifted = total_ref[cluster] + terms[place * vecs : (place + 1) * vecs]
            if given:
                shifted = shifted + given_ref[cluster]
            stacked = jnp.concatenate([block_ref[cluster], shifted], axis=0)
            stacked_ref[cluster] = stacked
            sums += dot_split(stacked, shifted)
    early = early_ref[...]
    crossed = sums[:vecs]
    products = jnp.concatenate(
        [crossed + early[:, vecs:], crossed, sums[vecs:], early[:, :vecs]], axis=1
    )
    for part in range(products_ref.shape[0]):
        products_ref[part] = products


def finish_kernel(point_count, products_ref, stacked_ref, next_ref, alpha_ref, beta_ref):
    clusters, vecs, size = next_ref.shape
    sums = products_ref[0]
    for part in range(1, products_ref.shape[0]):
        sums = sums + products_ref[part]
    sums = sums * (1.0 / point_count)
    alpha = sums[:, :vecs]
    crossed = sums[:, vecs : 2 * vecs]
    shifted = sums[:, 2 * vecs : 3 * vecs]
    block = sums[:, 3 * vecs :]
    alpha_ref[...] = alpha
    turned = alpha.T
    crossed = dot_exact(turned, crossed - 0.5 * dot_exact(block, alpha))
    gram = shifted - crossed - crossed.T
    rows = lax.broadcasted_iota(jnp.int32, (vecs, vecs), 0)
    columns = lax.broadcasted_iota(jnp.int32, (vecs, vecs), 1)
    unit = (rows == columns).astype(jnp.float32)
    work = jnp.concatenate([gram, unit], axis=1)
    row_ids = lax.broadcasted_iota(jnp.int32, (vecs, 1), 0)
    full = (vecs, 2 * vecs)
    row_full = lax.broadcasted_iota(jnp.int32, full, 0)
    for step in range(0, vecs - 2, 2):
        left = jnp.broadcast_to(work[:, step : step + 1], full)
        right = jnp.broadcast_to(work[:, step + 1 : step + 2], full)
        first, second = work[step : step + 1, :], work[step + 1 : step + 2, :]
        corner, side = left[step : step + 1, :], left[step + 1 : step + 2, :]
        other = right[step + 1 : step + 2, :]
        scale = 1.0 / (corner * other - side * side)
        first, second = (other * first - side * second) * scale, (corner * second - side * first) * scale
        below = row_full > step + 1
        work = work - jnp.where(below, left * first + right * second, 0.0)
    pivots = jnp.sum(work[:, :vecs] * unit, axis=1, keepdims=True)
    beside = (columns == rows + 1).astype(jnp.float32)
    ratios = jnp.sum(work[:, :vecs] * beside, axis=1, keepdims=True) / pivots
    taken = jnp.where(row_ids % 2 == 0, ratios, 0.0) * work
    work = work - jnp.concatenate([jnp.zeros((1, 2 * vecs), jnp.float32), taken[:-1]], axis=0)
    pivots = jnp.sum(work[:, :vecs] * unit, axis=1, keepdims=True)
    work = work * (1.0 / jnp.sqrt(pivots))
    beta_ref[...] = jnp.where(columns >= rows, work[:, :vecs], 0.0)
    inverse = work[:, vecs:]
    joint = jnp.concatenate([-dot_exact(inverse, turned), inverse], axis=1)
    for cluster in range(clusters):
        next_ref[cluster] = dot_exact(joint, stacked_ref[cluster])


def call(kernel, out_shape, operands, scratch=(), smem=0, smem_out=0, flops=0, vmem=20 << 20):
    def specs(total, scalars):
        places = [pltpu.SMEM] * scalars + [pltpu.VMEM] * (total - scalars)
        return [pl.BlockSpec(memory_space=place) for place in places]

    return pl.pallas_call(
        kernel,
        out_shape=out_shape,
        in_specs=specs(len(operands), smem),
        out_specs=specs(len(out_shape), smem_out),
        scratch_shapes=list(scratch),
        compiler_params=pltpu.CompilerParams(vmem_limit_bytes=vmem),
        cost_estimate=pl.CostEstimate(
            flops=flops, bytes_accessed=1 << 20, transcendentals=flops // 64
        ),
    )(*operands)


def passed(values, parts, step):
    pairs = [(index, index ^ step) for index in range(parts)]
    return lax.ppermute(values, "clus", pairs)


def spread(message, halved, parts):
    def group_of(steps, pieces):
        def owner_of(me, place):
            return me ^ steps[place]

        return owner_of, pieces

    if parts != 16:
        everything = lax.all_gather(message, "clus", axis=0, tiled=False)
        count = 8 if parts % 8 == 0 else 1
        yield
        for first in range(0, parts, count):
            yield (
                functools.partial(lambda first, me, place: first + place, first),
                [[everything[first + place]] for place in range(count)],
            )
        return
    along, inner, over = 2, 4, 12

    def held(values, token):
        return lax.optimization_barrier((values, token))[0]

    def fetched(values, step):
        return passed(values, parts, step)

    head, tail = (fetched(half, over) for half in halved)
    inward, sideways = fetched(message, inner), fetched(message, along)
    token = yield
    head, sideways = held((head, sideways), token)
    inner_head, side_head = fetched(head, inner), fetched(head, along)
    token = yield group_of([0], [[message]])
    tail, inward, side_head = held((tail, inward, side_head), token)
    side_tail, inner_tail = fetched(tail, along), fetched(tail, inner)
    last_head = fetched(side_head, inner)
    diagonal = fetched(inward, along)
    token = yield group_of([over, inner, along], [[head, tail], [inward], [sideways]])
    side_tail, diagonal, inner_head, inner_tail, last_head = held(
        (side_tail, diagonal, inner_head, inner_tail, last_head), token
    )
    last_tail = fetched(side_tail, inner)
    token = yield group_of(
        [inner ^ along, over ^ inner, over ^ along],
        [[diagonal], [inner_head, inner_tail], [side_head, side_tail]],
    )
    last_tail = held(last_tail, token)
    yield group_of([over ^ inner ^ along], [[last_head, last_tail]])


def local(
    block_vectors, prior_vectors, prior_beta, points, basis, scales, skeleton, near_pairs, far_ids
):
    clusters, vecs, size = block_vectors.shape
    rank = basis.shape[1]
    parts = lax.axis_size("clus")
    slots = near_pairs.shape[2]
    total_points = parts * clusters * size
    halves = clusters * rank // size
    rows = dict(layout_of(clusters, vecs, rank, size), slots=slots)
    core = 1
    shared = parts == 16
    targets = 2 if shared else 1
    wide = functools.partial(jax.ShapeDtypeStruct, dtype=jnp.float32)
    narrow = functools.partial(jax.ShapeDtypeStruct, dtype=jnp.bfloat16)

    asked = near_pairs.transpose(0, 2, 3, 1)
    message, *halved = call(
        functools.partial(prepare_kernel, rows),
        [narrow((rows["end"], size))] + [narrow((rows["end"] // 2, size))] * (2 if shared else 0),
        (
            block_vectors, basis, scales, points.transpose(1, 0, 2), skeleton.transpose(1, 0, 2),
            asked,
        ),
        vmem=56 << 20,
    )
    groups = spread(message, halved, parts)
    next(groups)
    own, lists = [message], [far_ids]
    if shared:
        own.append(passed(message, parts, core))
        lists.append(passed(far_ids, parts, core))
    lanes = -(-parts // 128) * 128
    blocks = parts * halves
    state = [wide((targets * clusters + 1, vecs, size)), wide((targets * halves, vecs, size))]
    total, far, early, left, far_left, counts, ids = call(
        functools.partial(local_kernel, rows, targets),
        state
        + [
            wide((vecs, 2 * vecs)),
            narrow((targets * clusters, size, feature_count)),
            narrow((targets * halves, size, feature_count)),
            wide((targets * blocks, clusters, size)),
            jax.ShapeDtypeStruct((targets, 8, lanes), jnp.int32),
        ],
        (*own, *lists, block_vectors, prior_vectors, prior_beta),
        flops=1 << 31,
    )

    def target_of(me, target):
        return me ^ (core * target)

    token, seen, sources = early, 0, parts // targets
    while seen < sources:
        owner_of, messages = groups.send(token)
        seen += len(messages)
        last = seen == sources
        devices = len(messages)
        entries = 2 * slots * devices * targets + unroll
        pieces = [piece for message_pieces in messages for piece in message_pieces]
        out_shape = state
        if last:
            out_shape = [wide((clusters, vecs, size)), wide((halves, vecs, size))]
            out_shape.append(wide((clusters + halves, vecs, size)))
        total, far, *given = call(
            functools.partial(
                add_kernel, rows, owner_of, target_of,
                [len(message_pieces) for message_pieces in messages], last,
            ),
            out_shape,
            [total, far, left, far_left, counts, ids] + pieces,
            scratch=[
                pltpu.VMEM((targets * clusters + 1, vecs, size), jnp.float32),
                pltpu.VMEM((targets * halves, vecs, size), jnp.float32),
                pltpu.VMEM((devices * clusters, vecs, size), jnp.bfloat16),
                pltpu.VMEM((devices * halves, vecs, size), jnp.bfloat16),
                pltpu.VMEM((devices * clusters, feature_count, size), jnp.bfloat16),
                pltpu.VMEM((devices * halves, feature_count, size), jnp.bfloat16),
                pltpu.VMEM((devices + targets, 8, lanes), jnp.int32),
                pltpu.SMEM((devices + targets, 8, lanes), jnp.int32),
                pltpu.SMEM((entries,), jnp.int32),
                pltpu.SMEM((entries,), jnp.int32),
                pltpu.SMEM((entries,), jnp.int32),
                pltpu.SemaphoreType.DMA,
            ],
            flops=devices << 28,
        )
        token = far
    given = given[0]
    if shared:
        given = passed(given, parts, core)
    stacked, products = call(
        functools.partial(combine_kernel, shared),
        [wide((clusters, 2 * vecs, size)), wide((parts, vecs, 4 * vecs))],
        (total, far, given, basis, scales, early, block_vectors),
        flops=1 << 28,
    )
    summed = lax.all_to_all(products, "clus", split_axis=0, concat_axis=0, tiled=True)
    return tuple(
        call(
            functools.partial(finish_kernel, total_points),
            [wide((clusters, vecs, size)), wide((vecs, vecs)), wide((vecs, vecs))],
            (summed, stacked),
        )
    )


def solution(mesh):
    placed = (
        P(("group", "clus"), None, None),
        P(("group", "clus"), None, None),
        P("group", None),
        P(("group", "clus"), None, None),
        P(("group", "clus"), None, None),
        P(("group", "clus"), None),
        P(("group", "clus"), None, None),
        P(("group", "clus"), None, None, None),
        P(("group", "clus"), None),
    )
    return jax.shard_map(
        local,
        mesh=mesh,
        in_specs=placed,
        out_specs=(P(("group", "clus"), None, None), P("group", None), P("group", None)),
        check_vma=False,
    )
```

```python
import functools
import math

import jax
import jax.numpy as jnp
from jax import lax
from jax.experimental import pallas as pl
from jax.experimental.pallas import tpu as pltpu
from jax.sharding import PartitionSpec as P

root_three = 1.7320508075688772
length_scale = 0.15
scale = root_three / length_scale * math.log2(math.e)
feature_count = 16
unroll = 16
NT = (((1,), (1,)), ((), ()))


def kernel_values(squared):
    squared = jnp.maximum(squared, 1e-9)
    distance = squared * lax.rsqrt(squared)
    decay = jnp.exp2(math.log2(math.log(2.0)) - distance)
    return (distance + 1.0 / math.log(2.0)) * decay


def dot_nt(left, right):
    return lax.dot_general(left, right, NT, preferred_element_type=jnp.float32)


def dot_exact(left, right, dims=(((1,), (0,)), ((), ()))):
    return lax.dot_general(
        left, right, dims, precision=lax.Precision.HIGHEST, preferred_element_type=jnp.float32
    )


def split(values):
    high = values.astype(jnp.bfloat16)
    return high, (values - high.astype(jnp.float32)).astype(jnp.bfloat16)


def dot_split(left, right):
    left_high, left_low = split(left)
    right_high, right_low = split(right)
    return dot_nt(
        jnp.concatenate([left_high, left_high, left_low], axis=1),
        jnp.concatenate([right_high, right_low, right_high], axis=1),
    )


def values_of(left_features, right_features):
    return kernel_values(jnp.dot(left_features, right_features, preferred_element_type=jnp.float32))


def tile_of(left_features, right_features):
    return values_of(left_features, right_features).astype(jnp.bfloat16)


def pieces_of(values):
    high = values.astype(jnp.bfloat16).astype(jnp.float32)
    rest = values - high
    middle = rest.astype(jnp.bfloat16).astype(jnp.float32)
    return [high, middle, rest - middle]


def norm_pieces(axes):
    norm = axes[0] * axes[0] + axes[1] * axes[1] + axes[2] * axes[2]
    return pieces_of(norm * (scale * scale))


def stack_rows(rows):
    rows = rows + [jnp.zeros_like(rows[0])] * (feature_count - len(rows))
    return jnp.transpose(jnp.stack(rows, axis=0), (1, 0, 2))


def left_rows(axes):
    one = jnp.ones_like(axes[0])
    return stack_rows([axis for axis in axes for _ in range(3)] + norm_pieces(axes) + [one] * 3)


def right_rows(axes):
    one = jnp.ones_like(axes[0])
    crossed = [piece for axis in axes for piece in pieces_of(axis * (-2.0 * scale * scale))]
    return stack_rows(crossed + [one] * 3 + norm_pieces(axes))


def layout_of(clusters, vecs, rank, size):
    halves = clusters * rank // size
    rows = {"sources": clusters * vecs}
    rows["points"] = rows["sources"] + halves * vecs
    rows["skeleton"] = rows["points"] + 3 * clusters
    rows["ids"] = -(-(rows["skeleton"] + 3 * halves) // 8) * 8
    rows["end"] = -(-(rows["ids"] + 8) // 16) * 16
    return rows


def prepare_kernel(
    rows, block_ref, basis_ref, scales_ref, points_ref, skeleton_ref, ids_ref, message_ref, *half_refs
):
    clusters, rank, size = basis_ref.shape
    vecs = block_ref.shape[1]
    per_row = size // rank
    halves = clusters // per_row
    for half in range(halves):
        pieces = []
        for place in range(per_row):
            cluster = half * per_row + place
            vectors = block_ref[cluster].astype(jnp.bfloat16)
            message_ref[cluster * vecs : (cluster + 1) * vecs, :] = vectors
            projected = dot_nt(vectors, basis_ref[cluster])
            pieces.append(projected * scales_ref[cluster : cluster + 1, :])
        start = rows["sources"] + half * vecs
        message_ref[start : start + vecs, :] = jnp.concatenate(pieces, axis=1).astype(jnp.bfloat16)
    for axis in range(3):
        start = rows["points"] + axis * clusters
        message_ref[start : start + clusters, :] = points_ref[axis]
    lines = []
    for axis in range(3):
        skeleton = skeleton_ref[axis].astype(jnp.float32)
        for half in range(halves):
            first = half * per_row
            lines.append(
                jnp.concatenate(
                    [skeleton[first + k : first + k + 1, :] for k in range(per_row)], axis=1
                )
            )
    lines.append(jnp.zeros((rows["ids"] - rows["skeleton"] - len(lines), size), jnp.float32))
    ids = jnp.concatenate([ids_ref[0, slot] for slot in range(ids_ref.shape[1])], axis=0)
    ids = ids.astype(jnp.float32)
    lines.append(
        jnp.concatenate([ids, jnp.zeros((ids.shape[0], size - ids.shape[1]), jnp.float32)], axis=1)
    )
    lines.append(jnp.zeros((rows["end"] - rows["ids"] - ids.shape[0], size), jnp.float32))
    message_ref[rows["skeleton"] :, :] = jnp.concatenate(lines, axis=0).astype(jnp.bfloat16)
    for place, half_ref in enumerate(half_refs):
        count = half_ref.shape[0]
        half_ref[...] = message_ref[place * count : (place + 1) * count, :]


def axes_of(values, start, count):
    return [values[start + k * count : start + (k + 1) * count] for k in range(3)]


def local_kernel(rows, targets, *refs):
    messages, far_refs, refs = refs[:targets], refs[targets : 2 * targets], refs[2 * targets :]
    (
        block_ref, prior_ref, beta_ref,
        total_ref, far_ref, early_ref, left_ref, far_left_ref, counts_ref, ids_ref,
    ) = refs
    clusters, vecs, size = block_ref.shape
    blocks = counts_ref.shape[0] // targets
    halves = far_left_ref.shape[0] // targets
    per_row = clusters // halves
    rank = size // per_row
    lanes = lax.broadcasted_iota(jnp.int32, (clusters, blocks * per_row), 1)
    row_ids = lax.broadcasted_iota(jnp.int32, (per_row, size), 0)
    widen = lax.div(lax.broadcasted_iota(jnp.int32, (per_row, size), 1), rank) == row_ids
    widen = widen.astype(jnp.bfloat16)
    for target in range(targets):
        tail = messages[target][rows["points"] :, :].astype(jnp.float32)
        axes = axes_of(tail, 0, clusters)
        left = left_rows(axes)
        for cluster in range(clusters):
            left_ref[target * clusters + cluster] = left[cluster].T.astype(jnp.bfloat16)
        if target == 0:
            right = right_rows(axes).astype(jnp.bfloat16)
        far_left = left_rows(axes_of(tail, rows["skeleton"] - rows["points"], halves))
        for half in range(halves):
            far_left_ref[target * halves + half] = far_left[half].T.astype(jnp.bfloat16)
        ids = tail[rows["ids"] - rows["points"] : rows["ids"] - rows["points"] + 8]
        ids_ref[target] = ids[:, : ids_ref.shape[2]].astype(jnp.int32)

        far_ids = far_refs[target][...]
        listed = jnp.zeros(lanes.shape, jnp.float32)
        for place in range(far_ids.shape[1]):
            listed += (far_ids[:, place : place + 1] == lanes).astype(jnp.float32)
        listed = listed.astype(jnp.bfloat16)
        for block in range(blocks):
            counts_ref[target * blocks + block] = jnp.dot(
                listed[:, block * per_row : (block + 1) * per_row], widen,
                preferred_element_type=jnp.float32,
            )

    beta = beta_ref[...]
    sums = jnp.zeros((vecs, 2 * vecs), jnp.float32)
    for cluster in range(clusters):
        tile = tile_of(left_ref[cluster], right[cluster])
        term = dot_nt(messages[0][cluster * vecs : (cluster + 1) * vecs, :], tile)
        shift = dot_exact(beta, prior_ref[cluster])
        total_ref[cluster] = term - shift
        block = block_ref[cluster]
        sums += dot_split(block, jnp.concatenate([block, shift], axis=0))
    early_ref[...] = sums
    total_ref[clusters:] = jnp.zeros((total_ref.shape[0] - clusters, vecs, size), jnp.float32)
    far_ref[...] = jnp.zeros_like(far_ref)


def add_kernel(rows, owner_of, target_of, pieces, chosen, given, *refs):
    total_in, far_in, left_ref, far_left_ref, counts_ref, own_ids_ref = refs[:6]
    count = sum(pieces)
    messages, refs = refs[6 : 6 + count], refs[6 + count :]
    outputs, refs = refs[: 1 if given else 2], refs[1 if given else 2 :]
    (
        total_ref, far_ref, vectors_ref, sources_ref, right_ref, far_right_ref, ids_ref,
        ids_scalar_ref, source_ref, own_ref, mirror_ref, copied,
    ) = refs
    devices = len(pieces)
    targets = own_ids_ref.shape[0]
    clusters = left_ref.shape[0] // targets
    size = left_ref.shape[1]
    sides = far_ref.shape[0]
    halves = sides // targets
    vecs = far_ref.shape[1]
    per_row = clusters // halves
    rank = size // per_row
    slots = rows["slots"]
    blocks = counts_ref.shape[0] // targets
    me = lax.axis_index("clus")
    owners = [owner_of(me, device) for device in range(devices)]

    for target in chosen:
        base = target * clusters
        total_ref[base : base + clusters] = total_in[base : base + clusters]
    far_ref[...] = far_in[...]
    total_ref[targets * clusters] = jnp.zeros((vecs, size), jnp.float32)
    start = 0
    for device, number in enumerate(pieces):
        first = 0
        for piece in messages[start : start + number]:
            upto = min(first + piece.shape[0], clusters * vecs)
            for row in range(first, upto, vecs):
                vectors_ref[device * clusters + row // vecs] = piece[row - first : row - first + vecs, :]
            before, first = first, first + piece.shape[0]
        rest = messages[start + number - 1]
        start += number
        offset = rows["sources"] - before
        for half in range(halves):
            sources_ref[device * halves + half] = rest[offset + half * vecs : offset + (half + 1) * vecs, :]
        tail = rest[rows["points"] - before :, :].astype(jnp.float32)
        right = right_rows(axes_of(tail, 0, clusters))
        right_ref[device * clusters : (device + 1) * clusters] = right.astype(jnp.bfloat16)
        right = right_rows(axes_of(tail, rows["skeleton"] - rows["points"], halves))
        far_right_ref[device * halves : (device + 1) * halves] = right.astype(jnp.bfloat16)
        ids = tail[rows["ids"] - rows["points"] : rows["ids"] - rows["points"] + 8]
        ids_ref[device] = ids[:, : ids_ref.shape[2]].astype(jnp.int32)
    for target in chosen:
        ids_ref[devices + target] = own_ids_ref[target]
    copy = pltpu.make_async_copy(ids_ref, ids_scalar_ref, copied)
    copy.start()

    chosen_sides = [target * halves + half for target in chosen for half in range(halves)]
    pair = 2 if devices % 2 == 0 else 1

    def far_step(turn, carry):
        terms = []
        for place in range(pair):
            device = turn * pair + place
            owner = owners[0]
            for known in range(1, devices):
                owner = jnp.where(device == known, owners[known], owner)
            for block in range(halves):
                features = far_right_ref[device * halves + block]
                sources = sources_ref[device * halves + block]
                for side in chosen_sides:
                    tile = values_of(far_left_ref[side], features)
                    weights = counts_ref[(side // halves) * blocks + owner * halves + block]
                    first = (side % halves) * per_row
                    weights = weights[first : first + per_row]
                    tile = tile.reshape(per_row, rank, size) * weights[:, None, :]
                    tile = tile.reshape(per_row * rank, size).astype(jnp.bfloat16)
                    terms.append((side, dot_nt(sources, tile)))
        for side, term in terms:
            far_ref[side] += term
        return carry

    lax.fori_loop(0, devices // pair, far_step, 0)

    copy.wait()
    live = jnp.int32(0)
    for device in range(devices):
        for target in chosen:
            asker = target_of(me, target)
            base = target * clusters
            for slot in range(slots):
                row, partner = 2 * slot, 2 * slot + 1
                asked = [ids_scalar_ref[devices + target, k, owners[device]] for k in (row, partner)]
                told = [ids_scalar_ref[device, k, asker] for k in (row, partner)]
                for alive, source, own, mirror in (
                    (asked[0], asked[1], asked[0], 0), (told[0], told[0], told[1], 1),
                ):
                    source_ref[live] = device * clusters + source
                    own_ref[live] = base + own
                    mirror_ref[live] = mirror
                    live = live + (alive >= 0).astype(jnp.int32)
    for extra in range(unroll):
        source_ref[live + extra] = 0
        own_ref[live + extra] = targets * clusters
        mirror_ref[live + extra] = 0

    def entry(place):
        source = source_ref[place]
        own = own_ref[place]
        tile = tile_of(left_ref[jnp.minimum(own, targets * clusters - 1)], right_ref[source])
        term = dot_nt(vectors_ref[source], tile)
        rounded = term.astype(jnp.bfloat16).astype(jnp.float32)
        return own, jnp.where(mirror_ref[place] > 0, rounded, term)

    def near_step(first, together):
        terms = [entry(first + place) for place in range(together)]
        for own, term in terms:
            total_ref[own] += term

    half, few = unroll // 2, unroll // 4
    turns = lax.div(live + (few - 1), unroll)

    def full_step(turn, carry):
        near_step(unroll * turn, unroll)
        return carry

    lax.fori_loop(0, turns, full_step, 0)
    done = unroll * turns
    more = live - done > few

    @pl.when(more)
    def _():
        near_step(done, half)

    done = done + jnp.where(more, half, 0)

    @pl.when(live > done)
    def _():
        near_step(done, few)

    first, upto = chosen[0], chosen[-1] + 1
    if given:
        outputs[0][:clusters] = total_ref[first * clusters : upto * clusters]
        outputs[0][clusters:] = far_ref[first * halves : upto * halves]
        return
    rest = outputs[0].shape[0] - (upto - first) * clusters
    outputs[0][...] = total_ref[first * clusters : upto * clusters + rest]
    outputs[1][...] = far_ref[first * halves : upto * halves]


def combine_kernel(
    given, total_ref, far_ref, given_ref, basis_ref, scales_ref, early_ref, block_ref,
    stacked_ref, products_ref
):
    clusters, vecs, size = total_ref.shape
    halves = far_ref.shape[0]
    per_row = clusters // halves
    rank = size // per_row
    sums = jnp.zeros((2 * vecs, vecs), jnp.float32)
    place_ids = lax.broadcasted_iota(jnp.int32, (per_row, vecs, size), 0)
    lane_ids = lax.broadcasted_iota(jnp.int32, (per_row, vecs, size), 2)
    own_lanes = lax.div(lane_ids, rank) == place_ids
    for side in range(halves):
        scales = scales_ref[side * per_row : (side + 1) * per_row, :]
        scales = jnp.concatenate([scales[place : place + 1] for place in range(per_row)], axis=1)
        gathered = far_ref[side]
        if given:
            gathered = gathered + given_ref[clusters + side]
        lifted = jnp.where(own_lanes, (gathered * scales)[None], 0.0)
        lifted = lifted.reshape(per_row * vecs, size).astype(jnp.bfloat16)
        basis = basis_ref[side * per_row : (side + 1) * per_row].reshape(per_row * rank, size)
        terms = jnp.dot(lifted, basis, preferred_element_type=jnp.float32)
        for place in range(per_row):
            cluster = side * per_row + place
            shifted = total_ref[cluster] + terms[place * vecs : (place + 1) * vecs]
            if given:
                shifted = shifted + given_ref[cluster]
            stacked = jnp.concatenate([block_ref[cluster], shifted], axis=0)
            stacked_ref[cluster] = stacked
            sums += dot_split(stacked, shifted)
    early = early_ref[...]
    crossed = sums[:vecs]
    products = jnp.concatenate(
        [crossed + early[:, vecs:], crossed, sums[vecs:], early[:, :vecs]], axis=1
    )
    for part in range(products_ref.shape[0]):
        products_ref[part] = products


def finish_kernel(point_count, products_ref, stacked_ref, next_ref, alpha_ref, beta_ref):
    clusters, vecs, size = next_ref.shape
    sums = products_ref[0]
    for part in range(1, products_ref.shape[0]):
        sums = sums + products_ref[part]
    sums = sums * (1.0 / point_count)
    alpha = sums[:, :vecs]
    crossed = sums[:, vecs : 2 * vecs]
    shifted = sums[:, 2 * vecs : 3 * vecs]
    block = sums[:, 3 * vecs :]
    alpha_ref[...] = alpha
    turned = alpha.T
    crossed = dot_exact(turned, crossed - 0.5 * dot_exact(block, alpha))
    gram = shifted - crossed - crossed.T
    rows = lax.broadcasted_iota(jnp.int32, (vecs, vecs), 0)
    columns = lax.broadcasted_iota(jnp.int32, (vecs, vecs), 1)
    unit = (rows == columns).astype(jnp.float32)
    work = jnp.concatenate([gram, unit], axis=1)
    row_ids = lax.broadcasted_iota(jnp.int32, (vecs, 1), 0)
    full = (vecs, 2 * vecs)
    row_full = lax.broadcasted_iota(jnp.int32, full, 0)
    for step in range(0, vecs - 2, 2):
        left = jnp.broadcast_to(work[:, step : step + 1], full)
        right = jnp.broadcast_to(work[:, step + 1 : step + 2], full)
        first, second = work[step : step + 1, :], work[step + 1 : step + 2, :]
        corner, side = left[step : step + 1, :], left[step + 1 : step + 2, :]
        other = right[step + 1 : step + 2, :]
        scale = 1.0 / (corner * other - side * side)
        first, second = (other * first - side * second) * scale, (corner * second - side * first) * scale
        below = row_full > step + 1
        work = work - jnp.where(below, left * first + right * second, 0.0)
    pivots = jnp.sum(work[:, :vecs] * unit, axis=1, keepdims=True)
    beside = (columns == rows + 1).astype(jnp.float32)
    ratios = jnp.sum(work[:, :vecs] * beside, axis=1, keepdims=True) / pivots
    taken = jnp.where(row_ids % 2 == 0, ratios, 0.0) * work
    work = work - jnp.concatenate([jnp.zeros((1, 2 * vecs), jnp.float32), taken[:-1]], axis=0)
    pivots = jnp.sum(work[:, :vecs] * unit, axis=1, keepdims=True)
    work = work * (1.0 / jnp.sqrt(pivots))
    beta_ref[...] = jnp.where(columns >= rows, work[:, :vecs], 0.0)
    inverse = work[:, vecs:]
    joint = jnp.concatenate([-dot_exact(inverse, turned), inverse], axis=1)
    for cluster in range(clusters):
        next_ref[cluster] = dot_exact(joint, stacked_ref[cluster])


def call(kernel, out_shape, operands, scratch=(), flops=0, vmem=20 << 20):
    held = pl.BlockSpec(memory_space=pltpu.VMEM)
    return pl.pallas_call(
        kernel,
        out_shape=out_shape,
        in_specs=[held] * len(operands),
        out_specs=[held] * len(out_shape),
        scratch_shapes=list(scratch),
        compiler_params=pltpu.CompilerParams(vmem_limit_bytes=vmem),
        cost_estimate=pl.CostEstimate(
            flops=flops, bytes_accessed=1 << 20, transcendentals=flops // 64
        ),
    )(*operands)


def passed(values, parts, step):
    pairs = [(index, index ^ step) for index in range(parts)]
    return lax.ppermute(values, "clus", pairs)


def spread(message, halved, parts):
    def group_of(steps, pieces):
        def owner_of(me, place):
            return me ^ steps[place]

        return owner_of, pieces

    if parts != 16:
        everything = lax.all_gather(message, "clus", axis=0, tiled=False)
        count = 8 if parts % 8 == 0 else 1
        yield
        for first in range(0, parts, count):
            yield (
                functools.partial(lambda first, me, place: first + place, first),
                [[everything[first + place]] for place in range(count)],
            )
        return
    along, inner, over = 2, 4, 12

    def held(values, token):
        return lax.optimization_barrier((values, token))[0]

    def fetched(values, step):
        return passed(values, parts, step)

    cut = message.shape[0] // 2
    sideways, inward, mirrored = (fetched(message, step) for step in (along, inner, over))
    yield
    token = yield group_of([0], [[message]])
    mirrored, inward, sideways = held((mirrored, inward, sideways), token)
    diagonal = [fetched(sideways[:cut], inner), fetched(inward[cut:], along)]
    mirrored_inward = fetched(mirrored, inner)
    mirrored_sideways = fetched(mirrored, along)
    token = yield group_of([over, inner, along], [[mirrored], [inward], [sideways]])
    mirrored_inward, mirrored_sideways = held((mirrored_inward, mirrored_sideways), token)
    last = [fetched(mirrored_sideways[:cut], inner), fetched(mirrored_inward[cut:], along)]
    token = yield group_of(
        [inner ^ along, over ^ inner, over ^ along],
        [diagonal, [mirrored_inward], [mirrored_sideways]],
    )
    last = held(last, token)
    yield group_of([over ^ inner ^ along], [last])


def local(
    block_vectors, prior_vectors, prior_beta, points, basis, scales, skeleton, near_pairs, far_ids
):
    clusters, vecs, size = block_vectors.shape
    rank = basis.shape[1]
    parts = lax.axis_size("clus")
    slots = near_pairs.shape[2]
    total_points = parts * clusters * size
    halves = clusters * rank // size
    rows = dict(layout_of(clusters, vecs, rank, size), slots=slots)
    core = 1
    shared = parts == 16
    targets = 2 if shared else 1
    wide = functools.partial(jax.ShapeDtypeStruct, dtype=jnp.float32)
    narrow = functools.partial(jax.ShapeDtypeStruct, dtype=jnp.bfloat16)

    asked = near_pairs.transpose(0, 2, 3, 1)
    message, *halved = call(
        functools.partial(prepare_kernel, rows),
        [narrow((rows["end"], size))] + [narrow((rows["end"] // 2, size))] * (2 if shared else 0),
        (
            block_vectors, basis, scales, points.transpose(1, 0, 2), skeleton.transpose(1, 0, 2),
            asked,
        ),
        vmem=56 << 20,
    )
    groups = spread(message, halved, parts)
    next(groups)
    own, lists = [message], [far_ids]
    if shared:
        own.append(passed(message, parts, core))
        lists.append(passed(far_ids, parts, core))
    lanes = -(-parts // 128) * 128
    blocks = parts * halves
    state = [wide((targets * clusters + 1, vecs, size)), wide((targets * halves, vecs, size))]
    total, far, early, left, far_left, counts, ids = call(
        functools.partial(local_kernel, rows, targets),
        state
        + [
            wide((vecs, 2 * vecs)),
            narrow((targets * clusters, size, feature_count)),
            narrow((targets * halves, size, feature_count)),
            wide((targets * blocks, clusters, size)),
            jax.ShapeDtypeStruct((targets, 8, lanes), jnp.int32),
        ],
        (*own, *lists, block_vectors, prior_vectors, prior_beta),
        flops=1 << 31,
    )

    def target_of(me, target):
        return me ^ (core * target)

    token, seen, sources = early, 0, parts // targets
    while seen < sources:
        owner_of, messages = groups.send(token)
        seen += len(messages)
        last = seen == sources
        devices = len(messages)
        entries = 2 * slots * devices * targets + unroll
        pieces = [piece for message_pieces in messages for piece in message_pieces]


        def add(total, chosen, out_shape, given=False):
            return call(
                functools.partial(
                    add_kernel, rows, owner_of, target_of,
                    [len(message_pieces) for message_pieces in messages], chosen, given,
                ),
                out_shape,
                [total, far, left, far_left, counts, ids] + pieces,
                scratch=[
                    pltpu.VMEM((targets * clusters + 1, vecs, size), jnp.float32),
                    pltpu.VMEM((targets * halves, vecs, size), jnp.float32),
                    pltpu.VMEM((devices * clusters, vecs, size), jnp.bfloat16),
                    pltpu.VMEM((devices * halves, vecs, size), jnp.bfloat16),
                    pltpu.VMEM((devices * clusters, feature_count, size), jnp.bfloat16),
                    pltpu.VMEM((devices * halves, feature_count, size), jnp.bfloat16),
                    pltpu.VMEM((devices + targets, 8, lanes), jnp.int32),
                    pltpu.SMEM((devices + targets, 8, lanes), jnp.int32),
                    pltpu.SMEM((entries,), jnp.int32),
                    pltpu.SMEM((entries,), jnp.int32),
                    pltpu.SMEM((entries,), jnp.int32),
                    pltpu.SemaphoreType.DMA,
                ],
                flops=devices << 28,
            )

        if not last:
            total, far = add(total, tuple(range(targets)), state)
            token = far
    given = far
    if shared:
        (given,) = add(total, (1,), [wide((clusters + halves, vecs, size))], True)
        total, given = lax.optimization_barrier((total, given))
        given = passed(given, parts, core)
    total, far = add(total, (0,), [wide((clusters, vecs, size)), wide((halves, vecs, size))])
    stacked, products = call(
        functools.partial(combine_kernel, shared),
        [wide((clusters, 2 * vecs, size)), wide((parts, vecs, 4 * vecs))],
        (total, far, given, basis, scales, early, block_vectors),
        flops=1 << 28,
    )
    summed = lax.all_to_all(products, "clus", split_axis=0, concat_axis=0, tiled=True)
    return tuple(
        call(
            functools.partial(finish_kernel, total_points),
            [wide((clusters, vecs, size)), wide((vecs, vecs)), wide((vecs, vecs))],
            (summed, stacked),
        )
    )


def solution(mesh):
    placed = (
        P(("group", "clus"), None, None),
        P(("group", "clus"), None, None),
        P("group", None),
        P(("group", "clus"), None, None),
        P(("group", "clus"), None, None),
        P(("group", "clus"), None),
        P(("group", "clus"), None, None),
        P(("group", "clus"), None, None, None),
        P(("group", "clus"), None),
    )
    return jax.shard_map(
        local,
        mesh=mesh,
        in_specs=placed,
        out_specs=(P(("group", "clus"), None, None), P("group", None), P("group", None)),
        check_vma=False,
    )
```

```python
import functools
import math

import jax
import jax.numpy as jnp
from jax import lax
from jax.experimental import pallas as pl
from jax.experimental.pallas import tpu as pltpu
from jax.sharding import PartitionSpec as P

root_three = 1.7320508075688772
length_scale = 0.15
scale = root_three / length_scale * math.log2(math.e)
feature_count = 16
unroll = 16
NT = (((1,), (1,)), ((), ()))


def kernel_values(squared):
    squared = jnp.maximum(squared, 1e-9)
    distance = squared * lax.rsqrt(squared)
    decay = jnp.exp2(math.log2(math.log(2.0)) - distance)
    return (distance + 1.0 / math.log(2.0)) * decay


def dot_nt(left, right):
    return lax.dot_general(left, right, NT, preferred_element_type=jnp.float32)


def dot_exact(left, right, dims=(((1,), (0,)), ((), ()))):
    return lax.dot_general(
        left, right, dims, precision=lax.Precision.HIGHEST, preferred_element_type=jnp.float32
    )


def split(values):
    high = values.astype(jnp.bfloat16)
    return high, (values - high.astype(jnp.float32)).astype(jnp.bfloat16)


def dot_split(left, right):
    left_high, left_low = split(left)
    right_high, right_low = split(right)
    return dot_nt(
        jnp.concatenate([left_high, left_high, left_low], axis=1),
        jnp.concatenate([right_high, right_low, right_high], axis=1),
    )


def values_of(left_features, right_features):
    return kernel_values(jnp.dot(left_features, right_features, preferred_element_type=jnp.float32))


def tile_of(left_features, right_features):
    return values_of(left_features, right_features).astype(jnp.bfloat16)


def pieces_of(values):
    high = values.astype(jnp.bfloat16).astype(jnp.float32)
    rest = values - high
    middle = rest.astype(jnp.bfloat16).astype(jnp.float32)
    return [high, middle, rest - middle]


def norm_pieces(axes):
    norm = axes[0] * axes[0] + axes[1] * axes[1] + axes[2] * axes[2]
    return pieces_of(norm * (scale * scale))


def stack_rows(rows):
    rows = rows + [jnp.zeros_like(rows[0])] * (feature_count - len(rows))
    return jnp.transpose(jnp.stack(rows, axis=0), (1, 0, 2))


def left_rows(axes):
    one = jnp.ones_like(axes[0])
    return stack_rows([axis for axis in axes for _ in range(3)] + norm_pieces(axes) + [one] * 3)


def right_rows(axes):
    one = jnp.ones_like(axes[0])
    crossed = [piece for axis in axes for piece in pieces_of(axis * (-2.0 * scale * scale))]
    return stack_rows(crossed + [one] * 3 + norm_pieces(axes))


def layout_of(clusters, vecs, rank, size):
    halves = clusters * rank // size
    rows = {"sources": clusters * vecs}
    rows["points"] = rows["sources"] + halves * vecs
    rows["skeleton"] = rows["points"] + 3 * clusters
    rows["ids"] = -(-(rows["skeleton"] + 3 * halves) // 8) * 8
    rows["end"] = -(-(rows["ids"] + 8) // 16) * 16
    return rows


def prepare_kernel(
    rows, block_ref, basis_ref, scales_ref, points_ref, skeleton_ref, ids_ref, message_ref, *half_refs
):
    clusters, rank, size = basis_ref.shape
    vecs = block_ref.shape[1]
    per_row = size // rank
    halves = clusters // per_row
    for half in range(halves):
        pieces = []
        for place in range(per_row):
            cluster = half * per_row + place
            vectors = block_ref[cluster].astype(jnp.bfloat16)
            message_ref[cluster * vecs : (cluster + 1) * vecs, :] = vectors
            projected = dot_nt(vectors, basis_ref[cluster])
            pieces.append(projected * scales_ref[cluster : cluster + 1, :])
        start = rows["sources"] + half * vecs
        message_ref[start : start + vecs, :] = jnp.concatenate(pieces, axis=1).astype(jnp.bfloat16)
    for axis in range(3):
        start = rows["points"] + axis * clusters
        message_ref[start : start + clusters, :] = points_ref[axis]
    lines = []
    for axis in range(3):
        skeleton = skeleton_ref[axis].astype(jnp.float32)
        for half in range(halves):
            first = half * per_row
            lines.append(
                jnp.concatenate(
                    [skeleton[first + k : first + k + 1, :] for k in range(per_row)], axis=1
                )
            )
    lines.append(jnp.zeros((rows["ids"] - rows["skeleton"] - len(lines), size), jnp.float32))
    ids = jnp.concatenate([ids_ref[0, slot] for slot in range(ids_ref.shape[1])], axis=0)
    ids = ids.astype(jnp.float32)
    lines.append(
        jnp.concatenate([ids, jnp.zeros((ids.shape[0], size - ids.shape[1]), jnp.float32)], axis=1)
    )
    lines.append(jnp.zeros((rows["end"] - rows["ids"] - ids.shape[0], size), jnp.float32))
    message_ref[rows["skeleton"] :, :] = jnp.concatenate(lines, axis=0).astype(jnp.bfloat16)
    for place, half_ref in enumerate(half_refs):
        count = half_ref.shape[0]
        half_ref[...] = message_ref[place * count : (place + 1) * count, :]


def axes_of(values, start, count):
    return [values[start + k * count : start + (k + 1) * count] for k in range(3)]


def local_kernel(rows, targets, *refs):
    messages, far_refs, refs = refs[:targets], refs[targets : 2 * targets], refs[2 * targets :]
    (
        block_ref, prior_ref, beta_ref,
        total_ref, far_ref, early_ref, left_ref, far_left_ref, counts_ref, ids_ref,
    ) = refs
    clusters, vecs, size = block_ref.shape
    blocks = counts_ref.shape[0] // targets
    halves = far_left_ref.shape[0] // targets
    per_row = clusters // halves
    rank = size // per_row
    lanes = lax.broadcasted_iota(jnp.int32, (clusters, blocks * per_row), 1)
    row_ids = lax.broadcasted_iota(jnp.int32, (per_row, size), 0)
    widen = lax.div(lax.broadcasted_iota(jnp.int32, (per_row, size), 1), rank) == row_ids
    widen = widen.astype(jnp.bfloat16)
    for target in range(targets):
        tail = messages[target][rows["points"] :, :].astype(jnp.float32)
        axes = axes_of(tail, 0, clusters)
        left = left_rows(axes)
        for cluster in range(clusters):
            left_ref[target * clusters + cluster] = left[cluster].T.astype(jnp.bfloat16)
        if target == 0:
            right = right_rows(axes).astype(jnp.bfloat16)
        far_left = left_rows(axes_of(tail, rows["skeleton"] - rows["points"], halves))
        for half in range(halves):
            far_left_ref[target * halves + half] = far_left[half].T.astype(jnp.bfloat16)
        ids = tail[rows["ids"] - rows["points"] : rows["ids"] - rows["points"] + 8]
        ids_ref[target] = ids[:, : ids_ref.shape[2]].astype(jnp.int32)

        far_ids = far_refs[target][...]
        listed = jnp.zeros(lanes.shape, jnp.float32)
        for place in range(far_ids.shape[1]):
            listed += (far_ids[:, place : place + 1] == lanes).astype(jnp.float32)
        listed = listed.astype(jnp.bfloat16)
        for block in range(blocks):
            counts_ref[target * blocks + block] = jnp.dot(
                listed[:, block * per_row : (block + 1) * per_row], widen,
                preferred_element_type=jnp.float32,
            )

    beta = beta_ref[...]
    sums = jnp.zeros((vecs, 2 * vecs), jnp.float32)
    for cluster in range(clusters):
        tile = tile_of(left_ref[cluster], right[cluster])
        term = dot_nt(messages[0][cluster * vecs : (cluster + 1) * vecs, :], tile)
        shift = dot_exact(beta, prior_ref[cluster])
        total_ref[cluster] = term - shift
        block = block_ref[cluster]
        sums += dot_split(block, jnp.concatenate([block, shift], axis=0))
    early_ref[...] = sums
    total_ref[clusters:] = jnp.zeros((total_ref.shape[0] - clusters, vecs, size), jnp.float32)
    far_ref[...] = jnp.zeros_like(far_ref)


def add_kernel(rows, owner_of, target_of, pieces, last, *refs):
    total_in, far_in, left_ref, far_left_ref, counts_ref, own_ids_ref = refs[:6]
    count = sum(pieces)
    messages, refs = refs[6 : 6 + count], refs[6 + count :]
    outputs, refs = refs[: 3 if last else 2], refs[3 if last else 2 :]
    (
        total_ref, far_ref, vectors_ref, sources_ref, right_ref, far_right_ref, ids_ref,
        ids_scalar_ref, source_ref, own_ref, mirror_ref, copied,
    ) = refs
    devices = len(pieces)
    targets = own_ids_ref.shape[0]
    clusters = left_ref.shape[0] // targets
    size = left_ref.shape[1]
    sides = far_ref.shape[0]
    halves = sides // targets
    vecs = far_ref.shape[1]
    per_row = clusters // halves
    rank = size // per_row
    slots = rows["slots"]
    blocks = counts_ref.shape[0] // targets
    me = lax.axis_index("clus")
    owners = [owner_of(me, device) for device in range(devices)]

    total_ref[...] = total_in[...]
    far_ref[...] = far_in[...]
    start = 0
    for device, number in enumerate(pieces):
        first = 0
        for piece in messages[start : start + number]:
            upto = min(first + piece.shape[0], clusters * vecs)
            for row in range(first, upto, vecs):
                vectors_ref[device * clusters + row // vecs] = piece[row - first : row - first + vecs, :]
            before, first = first, first + piece.shape[0]
        rest = messages[start + number - 1]
        start += number
        offset = rows["sources"] - before
        for half in range(halves):
            sources_ref[device * halves + half] = rest[offset + half * vecs : offset + (half + 1) * vecs, :]
        tail = rest[rows["points"] - before :, :].astype(jnp.float32)
        right = right_rows(axes_of(tail, 0, clusters))
        right_ref[device * clusters : (device + 1) * clusters] = right.astype(jnp.bfloat16)
        right = right_rows(axes_of(tail, rows["skeleton"] - rows["points"], halves))
        far_right_ref[device * halves : (device + 1) * halves] = right.astype(jnp.bfloat16)
        ids = tail[rows["ids"] - rows["points"] : rows["ids"] - rows["points"] + 8]
        ids_ref[device] = ids[:, : ids_ref.shape[2]].astype(jnp.int32)
    for target in range(targets):
        ids_ref[devices + target] = own_ids_ref[target]
    copy = pltpu.make_async_copy(ids_ref, ids_scalar_ref, copied)
    copy.start()

    pair = 2 if devices % 2 == 0 else 1

    def far_step(turn, carry):
        terms = []
        for place in range(pair):
            device = turn * pair + place
            owner = owners[0]
            for known in range(1, devices):
                owner = jnp.where(device == known, owners[known], owner)
            for block in range(halves):
                features = far_right_ref[device * halves + block]
                sources = sources_ref[device * halves + block]
                for side in range(sides):
                    tile = values_of(far_left_ref[side], features)
                    weights = counts_ref[(side // halves) * blocks + owner * halves + block]
                    first = (side % halves) * per_row
                    weights = weights[first : first + per_row]
                    tile = tile.reshape(per_row, rank, size) * weights[:, None, :]
                    tile = tile.reshape(per_row * rank, size).astype(jnp.bfloat16)
                    terms.append((side, dot_nt(sources, tile)))
        for side, term in terms:
            far_ref[side] += term
        return carry

    lax.fori_loop(0, devices // pair, far_step, 0)

    copy.wait()
    live = jnp.int32(0)
    for device in range(devices):
        for target in range(targets):
            asker = target_of(me, target)
            base = target * clusters
            for slot in range(slots):
                row, partner = 2 * slot, 2 * slot + 1
                asked = [ids_scalar_ref[devices + target, k, owners[device]] for k in (row, partner)]
                told = [ids_scalar_ref[device, k, asker] for k in (row, partner)]
                for alive, source, own, mirror in (
                    (asked[0], asked[1], asked[0], 0), (told[0], told[0], told[1], 1),
                ):
                    source_ref[live] = device * clusters + source
                    own_ref[live] = base + own
                    mirror_ref[live] = mirror
                    live = live + (alive >= 0).astype(jnp.int32)
    for extra in range(unroll):
        source_ref[live + extra] = 0
        own_ref[live + extra] = targets * clusters
        mirror_ref[live + extra] = 0

    def entry(place):
        source = source_ref[place]
        own = own_ref[place]
        tile = tile_of(left_ref[jnp.minimum(own, targets * clusters - 1)], right_ref[source])
        term = dot_nt(vectors_ref[source], tile)
        rounded = term.astype(jnp.bfloat16).astype(jnp.float32)
        return own, jnp.where(mirror_ref[place] > 0, rounded, term)

    def near_step(first, together):
        terms = [entry(first + place) for place in range(together)]
        for own, term in terms:
            total_ref[own] += term

    half, few = unroll // 2, unroll // 4
    turns = lax.div(live + (few - 1), unroll)

    def full_step(turn, carry):
        near_step(unroll * turn, unroll)
        return carry

    lax.fori_loop(0, turns, full_step, 0)
    done = unroll * turns
    more = live - done > few

    @pl.when(more)
    def _():
        near_step(done, half)

    done = done + jnp.where(more, half, 0)

    @pl.when(live > done)
    def _():
        near_step(done, few)

    if not last:
        outputs[0][...] = total_ref[...]
        outputs[1][...] = far_ref[...]
        return
    outputs[0][...] = total_ref[:clusters]
    outputs[1][...] = far_ref[:halves]
    outputs[2][:clusters] = total_ref[(targets - 1) * clusters : targets * clusters]
    outputs[2][clusters:] = far_ref[(targets - 1) * halves :]


def combine_kernel(
    given, total_ref, far_ref, given_ref, basis_ref, scales_ref, early_ref, block_ref,
    stacked_ref, products_ref
):
    clusters, vecs, size = total_ref.shape
    halves = far_ref.shape[0]
    per_row = clusters // halves
    rank = size // per_row
    sums = jnp.zeros((2 * vecs, vecs), jnp.float32)
    place_ids = lax.broadcasted_iota(jnp.int32, (per_row, vecs, size), 0)
    lane_ids = lax.broadcasted_iota(jnp.int32, (per_row, vecs, size), 2)
    own_lanes = lax.div(lane_ids, rank) == place_ids
    for side in range(halves):
        scales = scales_ref[side * per_row : (side + 1) * per_row, :]
        scales = jnp.concatenate([scales[place : place + 1] for place in range(per_row)], axis=1)
        gathered = far_ref[side]
        if given:
            gathered = gathered + given_ref[clusters + side]
        lifted = jnp.where(own_lanes, (gathered * scales)[None], 0.0)
        lifted = lifted.reshape(per_row * vecs, size).astype(jnp.bfloat16)
        basis = basis_ref[side * per_row : (side + 1) * per_row].reshape(per_row * rank, size)
        terms = jnp.dot(lifted, basis, preferred_element_type=jnp.float32)
        for place in range(per_row):
            cluster = side * per_row + place
            shifted = total_ref[cluster] + terms[place * vecs : (place + 1) * vecs]
            if given:
                shifted = shifted + given_ref[cluster]
            stacked = jnp.concatenate([block_ref[cluster], shifted], axis=0)
            stacked_ref[cluster] = stacked
            sums += dot_split(stacked, shifted)
    early = early_ref[...]
    crossed = sums[:vecs]
    products = jnp.concatenate(
        [crossed + early[:, vecs:], crossed, sums[vecs:], early[:, :vecs]], axis=1
    )
    for part in range(products_ref.shape[0]):
        products_ref[part] = products


def finish_kernel(point_count, products_ref, stacked_ref, next_ref, alpha_ref, beta_ref):
    clusters, vecs, size = next_ref.shape
    sums = products_ref[0]
    for part in range(1, products_ref.shape[0]):
        sums = sums + products_ref[part]
    sums = sums * (1.0 / point_count)
    alpha = sums[:, :vecs]
    crossed = sums[:, vecs : 2 * vecs]
    shifted = sums[:, 2 * vecs : 3 * vecs]
    block = sums[:, 3 * vecs :]
    alpha_ref[...] = alpha
    turned = alpha.T
    crossed = dot_exact(turned, crossed - 0.5 * dot_exact(block, alpha))
    gram = shifted - crossed - crossed.T
    rows = lax.broadcasted_iota(jnp.int32, (vecs, vecs), 0)
    columns = lax.broadcasted_iota(jnp.int32, (vecs, vecs), 1)
    unit = (rows == columns).astype(jnp.float32)
    work = jnp.concatenate([gram, unit], axis=1)
    row_ids = lax.broadcasted_iota(jnp.int32, (vecs, 1), 0)
    full = (vecs, 2 * vecs)
    row_full = lax.broadcasted_iota(jnp.int32, full, 0)
    for step in range(0, vecs - 2, 2):
        left = jnp.broadcast_to(work[:, step : step + 1], full)
        right = jnp.broadcast_to(work[:, step + 1 : step + 2], full)
        first, second = work[step : step + 1, :], work[step + 1 : step + 2, :]
        corner, side = left[step : step + 1, :], left[step + 1 : step + 2, :]
        other = right[step + 1 : step + 2, :]
        scale = 1.0 / (corner * other - side * side)
        first, second = (other * first - side * second) * scale, (corner * second - side * first) * scale
        below = row_full > step + 1
        work = work - jnp.where(below, left * first + right * second, 0.0)
    pivots = jnp.sum(work[:, :vecs] * unit, axis=1, keepdims=True)
    beside = (columns == rows + 1).astype(jnp.float32)
    ratios = jnp.sum(work[:, :vecs] * beside, axis=1, keepdims=True) / pivots
    taken = jnp.where(row_ids % 2 == 0, ratios, 0.0) * work
    work = work - jnp.concatenate([jnp.zeros((1, 2 * vecs), jnp.float32), taken[:-1]], axis=0)
    pivots = jnp.sum(work[:, :vecs] * unit, axis=1, keepdims=True)
    work = work * (1.0 / jnp.sqrt(pivots))
    beta_ref[...] = jnp.where(columns >= rows, work[:, :vecs], 0.0)
    inverse = work[:, vecs:]
    joint = jnp.concatenate([-dot_exact(inverse, turned), inverse], axis=1)
    for cluster in range(clusters):
        next_ref[cluster] = dot_exact(joint, stacked_ref[cluster])


def call(kernel, out_shape, operands, scratch=(), smem=0, smem_out=0, flops=0, vmem=20 << 20):
    def specs(total, scalars):
        places = [pltpu.SMEM] * scalars + [pltpu.VMEM] * (total - scalars)
        return [pl.BlockSpec(memory_space=place) for place in places]

    return pl.pallas_call(
        kernel,
        out_shape=out_shape,
        in_specs=specs(len(operands), smem),
        out_specs=specs(len(out_shape), smem_out),
        scratch_shapes=list(scratch),
        compiler_params=pltpu.CompilerParams(vmem_limit_bytes=vmem),
        cost_estimate=pl.CostEstimate(
            flops=flops, bytes_accessed=1 << 20, transcendentals=flops // 64
        ),
    )(*operands)


def passed(values, parts, step):
    pairs = [(index, index ^ step) for index in range(parts)]
    return lax.ppermute(values, "clus", pairs)


def spread(message, halved, parts):
    def group_of(steps, pieces):
        def owner_of(me, place):
            return me ^ steps[place]

        return owner_of, pieces

    if parts != 16:
        everything = lax.all_gather(message, "clus", axis=0, tiled=False)
        count = 8 if parts % 8 == 0 else 1
        yield
        for first in range(0, parts, count):
            yield (
                functools.partial(lambda first, me, place: first + place, first),
                [[everything[first + place]] for place in range(count)],
            )
        return
    along, inner, over = 2, 4, 12

    def held(values, token):
        return lax.optimization_barrier((values, token))[0]

    def fetched(values, step):
        return passed(values, parts, step)

    mirrored = fetched(message, over)
    inward = [fetched(half, inner) for half in halved]
    sideways = [fetched(half, along) for half in halved]
    cut = message.shape[0] // 2
    yield
    token = yield group_of([0], [[message]])
    mirrored, inward, sideways = held((mirrored, inward, sideways), token)
    mirrored_inward = fetched(mirrored, inner)
    mirrored_sideways = fetched(mirrored, along)
    diagonal = [fetched(sideways[0], inner), fetched(inward[1], along)]
    token = yield group_of([over, inner, along], [[mirrored], inward, sideways])
    mirrored_inward, mirrored_sideways = held((mirrored_inward, mirrored_sideways), token)
    last = [fetched(mirrored_sideways[:cut], inner), fetched(mirrored_inward[cut:], along)]
    token = yield group_of([over ^ inner, over ^ along], [[mirrored_inward], [mirrored_sideways]])
    last, diagonal = held((last, diagonal), token)
    yield group_of([inner ^ along, over ^ inner ^ along], [diagonal, last])


def local(
    block_vectors, prior_vectors, prior_beta, points, basis, scales, skeleton, near_pairs, far_ids
):
    clusters, vecs, size = block_vectors.shape
    rank = basis.shape[1]
    parts = lax.axis_size("clus")
    slots = near_pairs.shape[2]
    total_points = parts * clusters * size
    halves = clusters * rank // size
    rows = dict(layout_of(clusters, vecs, rank, size), slots=slots)
    core = 1
    shared = parts == 16
    targets = 2 if shared else 1
    wide = functools.partial(jax.ShapeDtypeStruct, dtype=jnp.float32)
    narrow = functools.partial(jax.ShapeDtypeStruct, dtype=jnp.bfloat16)

    asked = near_pairs.transpose(0, 2, 3, 1)
    message, *halved = call(
        functools.partial(prepare_kernel, rows),
        [narrow((rows["end"], size))] + [narrow((rows["end"] // 2, size))] * (2 if shared else 0),
        (
            block_vectors, basis, scales, points.transpose(1, 0, 2), skeleton.transpose(1, 0, 2),
            asked,
        ),
        vmem=56 << 20,
    )
    groups = spread(message, halved, parts)
    next(groups)
    own, lists = [message], [far_ids]
    if shared:
        own.append(passed(message, parts, core))
        lists.append(passed(far_ids, parts, core))
    lanes = -(-parts // 128) * 128
    blocks = parts * halves
    state = [wide((targets * clusters + 1, vecs, size)), wide((targets * halves, vecs, size))]
    total, far, early, left, far_left, counts, ids = call(
        functools.partial(local_kernel, rows, targets),
        state
        + [
            wide((vecs, 2 * vecs)),
            narrow((targets * clusters, size, feature_count)),
            narrow((targets * halves, size, feature_count)),
            wide((targets * blocks, clusters, size)),
            jax.ShapeDtypeStruct((targets, 8, lanes), jnp.int32),
        ],
        (*own, *lists, block_vectors, prior_vectors, prior_beta),
        flops=1 << 31,
    )

    def target_of(me, target):
        return me ^ (core * target)

    token, seen, sources = early, 0, parts // targets
    while seen < sources:
        owner_of, messages = groups.send(token)
        seen += len(messages)
        last = seen == sources
        devices = len(messages)
        entries = 2 * slots * devices * targets + unroll
        pieces = [piece for message_pieces in messages for piece in message_pieces]
        out_shape = state
        if last:
            out_shape = [wide((clusters, vecs, size)), wide((halves, vecs, size))]
            out_shape.append(wide((clusters + halves, vecs, size)))
        total, far, *given = call(
            functools.partial(
                add_kernel, rows, owner_of, target_of,
                [len(message_pieces) for message_pieces in messages], last,
            ),
            out_shape,
            [total, far, left, far_left, counts, ids] + pieces,
            scratch=[
                pltpu.VMEM((targets * clusters + 1, vecs, size), jnp.float32),
                pltpu.VMEM((targets * halves, vecs, size), jnp.float32),
                pltpu.VMEM((devices * clusters, vecs, size), jnp.bfloat16),
                pltpu.VMEM((devices * halves, vecs, size), jnp.bfloat16),
                pltpu.VMEM((devices * clusters, feature_count, size), jnp.bfloat16),
                pltpu.VMEM((devices * halves, feature_count, size), jnp.bfloat16),
                pltpu.VMEM((devices + targets, 8, lanes), jnp.int32),
                pltpu.SMEM((devices + targets, 8, lanes), jnp.int32),
                pltpu.SMEM((entries,), jnp.int32),
                pltpu.SMEM((entries,), jnp.int32),
                pltpu.SMEM((entries,), jnp.int32),
                pltpu.SemaphoreType.DMA,
            ],
            flops=devices << 28,
        )
        token = far
    given = given[0]
    if shared:
        given = passed(given, parts, core)
    stacked, products = call(
        functools.partial(combine_kernel, shared),
        [wide((clusters, 2 * vecs, size)), wide((parts, vecs, 4 * vecs))],
        (total, far, given, basis, scales, early, block_vectors),
        flops=1 << 28,
    )
    summed = lax.all_to_all(products, "clus", split_axis=0, concat_axis=0, tiled=True)
    return tuple(
        call(
            functools.partial(finish_kernel, total_points),
            [wide((clusters, vecs, size)), wide((vecs, vecs)), wide((vecs, vecs))],
            (summed, stacked),
        )
    )


def solution(mesh):
    placed = (
        P(("group", "clus"), None, None),
        P(("group", "clus"), None, None),
        P("group", None),
        P(("group", "clus"), None, None),
        P(("group", "clus"), None, None),
        P(("group", "clus"), None),
        P(("group", "clus"), None, None),
        P(("group", "clus"), None, None, None),
        P(("group", "clus"), None),
    )
    return jax.shard_map(
        local,
        mesh=mesh,
        in_specs=placed,
        out_specs=(P(("group", "clus"), None, None), P("group", None), P("group", None)),
        check_vma=False,
    )
```

```python
import functools
import math

import jax
import jax.numpy as jnp
from jax import lax
from jax.experimental import pallas as pl
from jax.experimental.pallas import tpu as pltpu
from jax.sharding import PartitionSpec as P

root_three = 1.7320508075688772
length_scale = 0.15
scale = root_three / length_scale * math.log2(math.e)
feature_count = 16
unroll = 16
NT = (((1,), (1,)), ((), ()))


def kernel_values(squared):
    squared = jnp.maximum(squared, 1e-9)
    distance = squared * lax.rsqrt(squared)
    decay = jnp.exp2(math.log2(math.log(2.0)) - distance)
    return (distance + 1.0 / math.log(2.0)) * decay


def dot_nt(left, right):
    return lax.dot_general(left, right, NT, preferred_element_type=jnp.float32)


def dot_exact(left, right, dims=(((1,), (0,)), ((), ()))):
    return lax.dot_general(
        left, right, dims, precision=lax.Precision.HIGHEST, preferred_element_type=jnp.float32
    )


def split(values):
    high = values.astype(jnp.bfloat16)
    return high, (values - high.astype(jnp.float32)).astype(jnp.bfloat16)


def dot_split(left, right):
    left_high, left_low = split(left)
    right_high, right_low = split(right)
    return dot_nt(
        jnp.concatenate([left_high, left_high, left_low], axis=1),
        jnp.concatenate([right_high, right_low, right_high], axis=1),
    )


def values_of(left_features, right_features):
    return kernel_values(jnp.dot(left_features, right_features, preferred_element_type=jnp.float32))


def tile_of(left_features, right_features):
    return values_of(left_features, right_features).astype(jnp.bfloat16)


def pieces_of(values):
    high = values.astype(jnp.bfloat16).astype(jnp.float32)
    rest = values - high
    middle = rest.astype(jnp.bfloat16).astype(jnp.float32)
    return [high, middle, rest - middle]


def norm_pieces(axes):
    norm = axes[0] * axes[0] + axes[1] * axes[1] + axes[2] * axes[2]
    return pieces_of(norm * (scale * scale))


def stack_rows(rows):
    rows = rows + [jnp.zeros_like(rows[0])] * (feature_count - len(rows))
    return jnp.transpose(jnp.stack(rows, axis=0), (1, 0, 2))


def left_rows(axes):
    one = jnp.ones_like(axes[0])
    return stack_rows([axis for axis in axes for _ in range(3)] + norm_pieces(axes) + [one] * 3)


def right_rows(axes):
    one = jnp.ones_like(axes[0])
    crossed = [piece for axis in axes for piece in pieces_of(axis * (-2.0 * scale * scale))]
    return stack_rows(crossed + [one] * 3 + norm_pieces(axes))


def layout_of(clusters, vecs, rank, size):
    halves = clusters * rank // size
    rows = {"sources": clusters * vecs}
    rows["points"] = rows["sources"] + halves * vecs
    rows["skeleton"] = rows["points"] + 3 * clusters
    rows["ids"] = -(-(rows["skeleton"] + 3 * halves) // 8) * 8
    rows["end"] = -(-(rows["ids"] + 8) // 16) * 16
    return rows


def prepare_kernel(
    rows, block_ref, basis_ref, scales_ref, points_ref, skeleton_ref, ids_ref, message_ref, *half_refs
):
    clusters, rank, size = basis_ref.shape
    vecs = block_ref.shape[1]
    per_row = size // rank
    halves = clusters // per_row
    for half in range(halves):
        pieces = []
        for place in range(per_row):
            cluster = half * per_row + place
            vectors = block_ref[cluster].astype(jnp.bfloat16)
            message_ref[cluster * vecs : (cluster + 1) * vecs, :] = vectors
            projected = dot_nt(vectors, basis_ref[cluster])
            pieces.append(projected * scales_ref[cluster : cluster + 1, :])
        start = rows["sources"] + half * vecs
        message_ref[start : start + vecs, :] = jnp.concatenate(pieces, axis=1).astype(jnp.bfloat16)
    for axis in range(3):
        start = rows["points"] + axis * clusters
        message_ref[start : start + clusters, :] = points_ref[axis]
    lines = []
    for axis in range(3):
        skeleton = skeleton_ref[axis].astype(jnp.float32)
        for half in range(halves):
            first = half * per_row
            lines.append(
                jnp.concatenate(
                    [skeleton[first + k : first + k + 1, :] for k in range(per_row)], axis=1
                )
            )
    lines.append(jnp.zeros((rows["ids"] - rows["skeleton"] - len(lines), size), jnp.float32))
    ids = jnp.concatenate([ids_ref[0, slot] for slot in range(ids_ref.shape[1])], axis=0)
    ids = ids.astype(jnp.float32)
    lines.append(
        jnp.concatenate([ids, jnp.zeros((ids.shape[0], size - ids.shape[1]), jnp.float32)], axis=1)
    )
    lines.append(jnp.zeros((rows["end"] - rows["ids"] - ids.shape[0], size), jnp.float32))
    message_ref[rows["skeleton"] :, :] = jnp.concatenate(lines, axis=0).astype(jnp.bfloat16)
    for place, half_ref in enumerate(half_refs):
        count = half_ref.shape[0]
        half_ref[...] = message_ref[place * count : (place + 1) * count, :]


def axes_of(values, start, count):
    return [values[start + k * count : start + (k + 1) * count] for k in range(3)]


def local_kernel(rows, targets, *refs):
    messages, far_refs, refs = refs[:targets], refs[targets : 2 * targets], refs[2 * targets :]
    (
        block_ref, prior_ref, beta_ref,
        total_ref, far_ref, early_ref, left_ref, far_left_ref, counts_ref, ids_ref,
    ) = refs
    clusters, vecs, size = block_ref.shape
    blocks = counts_ref.shape[0] // targets
    halves = far_left_ref.shape[0] // targets
    per_row = clusters // halves
    rank = size // per_row
    lanes = lax.broadcasted_iota(jnp.int32, (clusters, blocks * per_row), 1)
    row_ids = lax.broadcasted_iota(jnp.int32, (per_row, size), 0)
    widen = lax.div(lax.broadcasted_iota(jnp.int32, (per_row, size), 1), rank) == row_ids
    widen = widen.astype(jnp.bfloat16)
    for target in range(targets):
        tail = messages[target][rows["points"] :, :].astype(jnp.float32)
        axes = axes_of(tail, 0, clusters)
        left = left_rows(axes)
        for cluster in range(clusters):
            left_ref[target * clusters + cluster] = left[cluster].T.astype(jnp.bfloat16)
        if target == 0:
            right = right_rows(axes).astype(jnp.bfloat16)
        far_left = left_rows(axes_of(tail, rows["skeleton"] - rows["points"], halves))
        for half in range(halves):
            far_left_ref[target * halves + half] = far_left[half].T.astype(jnp.bfloat16)
        ids = tail[rows["ids"] - rows["points"] : rows["ids"] - rows["points"] + 8]
        ids_ref[target] = ids[:, : ids_ref.shape[2]].astype(jnp.int32)

        far_ids = far_refs[target][...]
        listed = jnp.zeros(lanes.shape, jnp.float32)
        for place in range(far_ids.shape[1]):
            listed += (far_ids[:, place : place + 1] == lanes).astype(jnp.float32)
        listed = listed.astype(jnp.bfloat16)
        for block in range(blocks):
            counts_ref[target * blocks + block] = jnp.dot(
                listed[:, block * per_row : (block + 1) * per_row], widen,
                preferred_element_type=jnp.float32,
            )

    beta = beta_ref[...]
    sums = jnp.zeros((vecs, 2 * vecs), jnp.float32)
    for cluster in range(clusters):
        tile = tile_of(left_ref[cluster], right[cluster])
        term = dot_nt(messages[0][cluster * vecs : (cluster + 1) * vecs, :], tile)
        shift = dot_exact(beta, prior_ref[cluster])
        total_ref[cluster] = term - shift
        block = block_ref[cluster]
        sums += dot_split(block, jnp.concatenate([block, shift], axis=0))
    early_ref[...] = sums
    total_ref[clusters:] = jnp.zeros((total_ref.shape[0] - clusters, vecs, size), jnp.float32)
    far_ref[...] = jnp.zeros_like(far_ref)


def add_kernel(rows, owner_of, target_of, pieces, last, *refs):
    total_in, far_in, left_ref, far_left_ref, counts_ref, own_ids_ref = refs[:6]
    count = sum(pieces)
    messages, refs = refs[6 : 6 + count], refs[6 + count :]
    outputs, refs = refs[: 3 if last else 2], refs[3 if last else 2 :]
    (
        total_ref, far_ref, vectors_ref, sources_ref, right_ref, far_right_ref, ids_ref,
        ids_scalar_ref, source_ref, own_ref, mirror_ref, copied,
    ) = refs
    devices = len(pieces)
    targets = own_ids_ref.shape[0]
    clusters = left_ref.shape[0] // targets
    size = left_ref.shape[1]
    sides = far_ref.shape[0]
    halves = sides // targets
    vecs = far_ref.shape[1]
    per_row = clusters // halves
    rank = size // per_row
    slots = rows["slots"]
    blocks = counts_ref.shape[0] // targets
    me = lax.axis_index("clus")
    owners = [owner_of(me, device) for device in range(devices)]

    total_ref[...] = total_in[...]
    far_ref[...] = far_in[...]
    start = 0
    for device, number in enumerate(pieces):
        first = 0
        for piece in messages[start : start + number]:
            upto = min(first + piece.shape[0], clusters * vecs)
            for row in range(first, upto, vecs):
                vectors_ref[device * clusters + row // vecs] = piece[row - first : row - first + vecs, :]
            before, first = first, first + piece.shape[0]
        rest = messages[start + number - 1]
        start += number
        offset = rows["sources"] - before
        for half in range(halves):
            sources_ref[device * halves + half] = rest[offset + half * vecs : offset + (half + 1) * vecs, :]
        tail = rest[rows["points"] - before :, :].astype(jnp.float32)
        right = right_rows(axes_of(tail, 0, clusters))
        right_ref[device * clusters : (device + 1) * clusters] = right.astype(jnp.bfloat16)
        right = right_rows(axes_of(tail, rows["skeleton"] - rows["points"], halves))
        far_right_ref[device * halves : (device + 1) * halves] = right.astype(jnp.bfloat16)
        ids = tail[rows["ids"] - rows["points"] : rows["ids"] - rows["points"] + 8]
        ids_ref[device] = ids[:, : ids_ref.shape[2]].astype(jnp.int32)
    for target in range(targets):
        ids_ref[devices + target] = own_ids_ref[target]
    copy = pltpu.make_async_copy(ids_ref, ids_scalar_ref, copied)
    copy.start()

    pair = 2 if targets == 1 and devices % 2 == 0 else 1

    def far_step(turn, carry):
        terms = []
        for place in range(pair):
            device = turn * pair + place
            owner = owners[0]
            for known in range(1, devices):
                owner = jnp.where(device == known, owners[known], owner)
            for block in range(halves):
                features = far_right_ref[device * halves + block]
                sources = sources_ref[device * halves + block]
                for side in range(sides):
                    tile = values_of(far_left_ref[side], features)
                    weights = counts_ref[(side // halves) * blocks + owner * halves + block]
                    first = (side % halves) * per_row
                    weights = weights[first : first + per_row]
                    tile = tile.reshape(per_row, rank, size) * weights[:, None, :]
                    tile = tile.reshape(per_row * rank, size).astype(jnp.bfloat16)
                    terms.append((side, dot_nt(sources, tile)))
        for side, term in terms:
            far_ref[side] += term
        return carry

    lax.fori_loop(0, devices // pair, far_step, 0)

    copy.wait()
    live = jnp.int32(0)
    for device in range(devices):
        for target in range(targets):
            asker = target_of(me, target)
            base = target * clusters
            for slot in range(slots):
                row, partner = 2 * slot, 2 * slot + 1
                asked = [ids_scalar_ref[devices + target, k, owners[device]] for k in (row, partner)]
                told = [ids_scalar_ref[device, k, asker] for k in (row, partner)]
                for alive, source, own, mirror in (
                    (asked[0], asked[1], asked[0], 0), (told[0], told[0], told[1], 1),
                ):
                    source_ref[live] = device * clusters + source
                    own_ref[live] = base + own
                    mirror_ref[live] = mirror
                    live = live + (alive >= 0).astype(jnp.int32)
    for extra in range(unroll):
        source_ref[live + extra] = 0
        own_ref[live + extra] = targets * clusters
        mirror_ref[live + extra] = 0

    def entry(place):
        source = source_ref[place]
        own = own_ref[place]
        tile = tile_of(left_ref[jnp.minimum(own, targets * clusters - 1)], right_ref[source])
        term = dot_nt(vectors_ref[source], tile)
        rounded = term.astype(jnp.bfloat16).astype(jnp.float32)
        return own, jnp.where(mirror_ref[place] > 0, rounded, term)

    def near_step(first, together):
        terms = [entry(first + place) for place in range(together)]
        for own, term in terms:
            total_ref[own] += term

    half, few = unroll // 2, unroll // 4
    turns = lax.div(live + (few - 1), unroll)

    def full_step(turn, carry):
        near_step(unroll * turn, unroll)
        return carry

    lax.fori_loop(0, turns, full_step, 0)
    done = unroll * turns
    more = live - done > few

    @pl.when(more)
    def _():
        near_step(done, half)

    done = done + jnp.where(more, half, 0)

    @pl.when(live > done)
    def _():
        near_step(done, few)

    if not last:
        outputs[0][...] = total_ref[...]
        outputs[1][...] = far_ref[...]
        return
    outputs[0][...] = total_ref[:clusters]
    outputs[1][...] = far_ref[:halves]
    outputs[2][:clusters] = total_ref[(targets - 1) * clusters : targets * clusters]
    outputs[2][clusters:] = far_ref[(targets - 1) * halves :]


def combine_kernel(
    given, total_ref, far_ref, given_ref, basis_ref, scales_ref, early_ref, block_ref,
    stacked_ref, products_ref
):
    clusters, vecs, size = total_ref.shape
    halves = far_ref.shape[0]
    per_row = clusters // halves
    rank = size // per_row
    sums = jnp.zeros((2 * vecs, vecs), jnp.float32)
    place_ids = lax.broadcasted_iota(jnp.int32, (per_row, vecs, size), 0)
    lane_ids = lax.broadcasted_iota(jnp.int32, (per_row, vecs, size), 2)
    own_lanes = lax.div(lane_ids, rank) == place_ids
    for side in range(halves):
        scales = scales_ref[side * per_row : (side + 1) * per_row, :]
        scales = jnp.concatenate([scales[place : place + 1] for place in range(per_row)], axis=1)
        gathered = far_ref[side]
        if given:
            gathered = gathered + given_ref[clusters + side]
        lifted = jnp.where(own_lanes, (gathered * scales)[None], 0.0)
        lifted = lifted.reshape(per_row * vecs, size).astype(jnp.bfloat16)
        basis = basis_ref[side * per_row : (side + 1) * per_row].reshape(per_row * rank, size)
        terms = jnp.dot(lifted, basis, preferred_element_type=jnp.float32)
        for place in range(per_row):
            cluster = side * per_row + place
            shifted = total_ref[cluster] + terms[place * vecs : (place + 1) * vecs]
            if given:
                shifted = shifted + given_ref[cluster]
            stacked = jnp.concatenate([block_ref[cluster], shifted], axis=0)
            stacked_ref[cluster] = stacked
            sums += dot_split(stacked, shifted)
    early = early_ref[...]
    crossed = sums[:vecs]
    products = jnp.concatenate(
        [crossed + early[:, vecs:], crossed, sums[vecs:], early[:, :vecs]], axis=1
    )
    for part in range(products_ref.shape[0]):
        products_ref[part] = products


def finish_kernel(point_count, products_ref, stacked_ref, next_ref, alpha_ref, beta_ref):
    clusters, vecs, size = next_ref.shape
    sums = products_ref[0]
    for part in range(1, products_ref.shape[0]):
        sums = sums + products_ref[part]
    sums = sums * (1.0 / point_count)
    alpha = sums[:, :vecs]
    crossed = sums[:, vecs : 2 * vecs]
    shifted = sums[:, 2 * vecs : 3 * vecs]
    block = sums[:, 3 * vecs :]
    alpha_ref[...] = alpha
    turned = alpha.T
    crossed = dot_exact(turned, crossed - 0.5 * dot_exact(block, alpha))
    gram = shifted - crossed - crossed.T
    rows = lax.broadcasted_iota(jnp.int32, (vecs, vecs), 0)
    columns = lax.broadcasted_iota(jnp.int32, (vecs, vecs), 1)
    unit = (rows == columns).astype(jnp.float32)
    work = jnp.concatenate([gram, unit], axis=1)
    row_ids = lax.broadcasted_iota(jnp.int32, (vecs, 1), 0)
    full = (vecs, 2 * vecs)
    row_full = lax.broadcasted_iota(jnp.int32, full, 0)
    for step in range(0, vecs - 2, 2):
        left = jnp.broadcast_to(work[:, step : step + 1], full)
        right = jnp.broadcast_to(work[:, step + 1 : step + 2], full)
        first, second = work[step : step + 1, :], work[step + 1 : step + 2, :]
        corner, side = left[step : step + 1, :], left[step + 1 : step + 2, :]
        other = right[step + 1 : step + 2, :]
        scale = 1.0 / (corner * other - side * side)
        first, second = (other * first - side * second) * scale, (corner * second - side * first) * scale
        below = row_full > step + 1
        work = work - jnp.where(below, left * first + right * second, 0.0)
    pivots = jnp.sum(work[:, :vecs] * unit, axis=1, keepdims=True)
    beside = (columns == rows + 1).astype(jnp.float32)
    ratios = jnp.sum(work[:, :vecs] * beside, axis=1, keepdims=True) / pivots
    taken = jnp.where(row_ids % 2 == 0, ratios, 0.0) * work
    work = work - jnp.concatenate([jnp.zeros((1, 2 * vecs), jnp.float32), taken[:-1]], axis=0)
    pivots = jnp.sum(work[:, :vecs] * unit, axis=1, keepdims=True)
    work = work * (1.0 / jnp.sqrt(pivots))
    beta_ref[...] = jnp.where(columns >= rows, work[:, :vecs], 0.0)
    inverse = work[:, vecs:]
    joint = jnp.concatenate([-dot_exact(inverse, turned), inverse], axis=1)
    for cluster in range(clusters):
        next_ref[cluster] = dot_exact(joint, stacked_ref[cluster])


def call(kernel, out_shape, operands, scratch=(), smem=0, smem_out=0, flops=0, vmem=20 << 20):
    def specs(total, scalars):
        places = [pltpu.SMEM] * scalars + [pltpu.VMEM] * (total - scalars)
        return [pl.BlockSpec(memory_space=place) for place in places]

    return pl.pallas_call(
        kernel,
        out_shape=out_shape,
        in_specs=specs(len(operands), smem),
        out_specs=specs(len(out_shape), smem_out),
        scratch_shapes=list(scratch),
        compiler_params=pltpu.CompilerParams(vmem_limit_bytes=vmem),
        cost_estimate=pl.CostEstimate(
            flops=flops, bytes_accessed=1 << 20, transcendentals=flops // 64
        ),
    )(*operands)


def passed(values, parts, step):
    pairs = [(index, index ^ step) for index in range(parts)]
    return lax.ppermute(values, "clus", pairs)


def spread(message, halved, parts):
    def group_of(steps, pieces):
        def owner_of(me, place):
            return me ^ steps[place]

        return owner_of, pieces

    if parts != 16:
        everything = lax.all_gather(message, "clus", axis=0, tiled=False)
        count = 8 if parts % 8 == 0 else 1
        yield
        for first in range(0, parts, count):
            yield (
                functools.partial(lambda first, me, place: first + place, first),
                [[everything[first + place]] for place in range(count)],
            )
        return
    along, inner, over = 2, 4, 12

    def held(values, token):
        return lax.optimization_barrier((values, token))[0]

    def fetched(values, step):
        return passed(values, parts, step)

    mirrored = fetched(message, over)
    inward = [fetched(half, inner) for half in halved]
    sideways = [fetched(half, along) for half in halved]
    cut = message.shape[0] // 2
    yield
    token = yield group_of([0], [[message]])
    mirrored, inward, sideways = held((mirrored, inward, sideways), token)
    mirrored_inward = fetched(mirrored, inner)
    mirrored_sideways = fetched(mirrored, along)
    diagonal = [fetched(sideways[0], inner), fetched(inward[1], along)]
    token = yield group_of([over, inner, along], [[mirrored], inward, sideways])
    mirrored_inward, mirrored_sideways = held((mirrored_inward, mirrored_sideways), token)
    last = [fetched(mirrored_sideways[:cut], inner), fetched(mirrored_inward[cut:], along)]
    token = yield group_of([over ^ inner, over ^ along], [[mirrored_inward], [mirrored_sideways]])
    last, diagonal = held((last, diagonal), token)
    yield group_of([inner ^ along, over ^ inner ^ along], [diagonal, last])


def local(
    block_vectors, prior_vectors, prior_beta, points, basis, scales, skeleton, near_pairs, far_ids
):
    clusters, vecs, size = block_vectors.shape
    rank = basis.shape[1]
    parts = lax.axis_size("clus")
    slots = near_pairs.shape[2]
    total_points = parts * clusters * size
    halves = clusters * rank // size
    rows = dict(layout_of(clusters, vecs, rank, size), slots=slots)
    core = 1
    shared = parts == 16
    targets = 2 if shared else 1
    wide = functools.partial(jax.ShapeDtypeStruct, dtype=jnp.float32)
    narrow = functools.partial(jax.ShapeDtypeStruct, dtype=jnp.bfloat16)

    asked = near_pairs.transpose(0, 2, 3, 1)
    message, *halved = call(
        functools.partial(prepare_kernel, rows),
        [narrow((rows["end"], size))] + [narrow((rows["end"] // 2, size))] * (2 if shared else 0),
        (
            block_vectors, basis, scales, points.transpose(1, 0, 2), skeleton.transpose(1, 0, 2),
            asked,
        ),
        vmem=56 << 20,
    )
    groups = spread(message, halved, parts)
    next(groups)
    own, lists = [message], [far_ids]
    if shared:
        own.append(passed(message, parts, core))
        lists.append(passed(far_ids, parts, core))
    lanes = -(-parts // 128) * 128
    blocks = parts * halves
    state = [wide((targets * clusters + 1, vecs, size)), wide((targets * halves, vecs, size))]
    total, far, early, left, far_left, counts, ids = call(
        functools.partial(local_kernel, rows, targets),
        state
        + [
            wide((vecs, 2 * vecs)),
            narrow((targets * clusters, size, feature_count)),
            narrow((targets * halves, size, feature_count)),
            wide((targets * blocks, clusters, size)),
            jax.ShapeDtypeStruct((targets, 8, lanes), jnp.int32),
        ],
        (*own, *lists, block_vectors, prior_vectors, prior_beta),
        flops=1 << 31,
    )

    def target_of(me, target):
        return me ^ (core * target)

    token, seen, sources = early, 0, parts // targets
    while seen < sources:
        owner_of, messages = groups.send(token)
        seen += len(messages)
        last = seen == sources
        devices = len(messages)
        entries = 2 * slots * devices * targets + unroll
        pieces = [piece for message_pieces in messages for piece in message_pieces]
        out_shape = state
        if last:
            out_shape = [wide((clusters, vecs, size)), wide((halves, vecs, size))]
            out_shape.append(wide((clusters + halves, vecs, size)))
        total, far, *given = call(
            functools.partial(
                add_kernel, rows, owner_of, target_of,
                [len(message_pieces) for message_pieces in messages], last,
            ),
            out_shape,
            [total, far, left, far_left, counts, ids] + pieces,
            scratch=[
                pltpu.VMEM((targets * clusters + 1, vecs, size), jnp.float32),
                pltpu.VMEM((targets * halves, vecs, size), jnp.float32),
                pltpu.VMEM((devices * clusters, vecs, size), jnp.bfloat16),
                pltpu.VMEM((devices * halves, vecs, size), jnp.bfloat16),
                pltpu.VMEM((devices * clusters, feature_count, size), jnp.bfloat16),
                pltpu.VMEM((devices * halves, feature_count, size), jnp.bfloat16),
                pltpu.VMEM((devices + targets, 8, lanes), jnp.int32),
                pltpu.SMEM((devices + targets, 8, lanes), jnp.int32),
                pltpu.SMEM((entries,), jnp.int32),
                pltpu.SMEM((entries,), jnp.int32),
                pltpu.SMEM((entries,), jnp.int32),
                pltpu.SemaphoreType.DMA,
            ],
            flops=devices << 28,
        )
        token = far
    given = given[0]
    if shared:
        given = passed(given, parts, core)
    stacked, products = call(
        functools.partial(combine_kernel, shared),
        [wide((clusters, 2 * vecs, size)), wide((parts, vecs, 4 * vecs))],
        (total, far, given, basis, scales, early, block_vectors),
        flops=1 << 28,
    )
    summed = lax.all_to_all(products, "clus", split_axis=0, concat_axis=0, tiled=True)
    return tuple(
        call(
            functools.partial(finish_kernel, total_points),
            [wide((clusters, vecs, size)), wide((vecs, vecs)), wide((vecs, vecs))],
            (summed, stacked),
        )
    )


def solution(mesh):
    placed = (
        P(("group", "clus"), None, None),
        P(("group", "clus"), None, None),
        P("group", None),
        P(("group", "clus"), None, None),
        P(("group", "clus"), None, None),
        P(("group", "clus"), None),
        P(("group", "clus"), None, None),
        P(("group", "clus"), None, None, None),
        P(("group", "clus"), None),
    )
    return jax.shard_map(
        local,
        mesh=mesh,
        in_specs=placed,
        out_specs=(P(("group", "clus"), None, None), P("group", None), P("group", None)),
        check_vma=False,
    )
```
